256 devices in a mesh: dp: 4 (over y), expert: 64 (over z, x, core).
Axes of the slice: x: 4, y: 4, z: 8, core: 2. Of those that a mesh axis runs over, the one named last changes fastest.
Arguments:
- queries: bfloat16 [8, 8192, 2048], P('dp', 'expert'), may hold values from -36 to 36
- key_rows: bfloat16 [8, 8192, 2048], P('dp', 'expert'), may hold values from -14 to 14
- value_rows: bfloat16 [8, 8192, 2048], P('dp', 'expert'), may hold values from -8 to 8
- contig_lengths: int32 [8, 64], replicated, may hold values from 1 to 256, as said below
- row_target: int32 [8], replicated, may hold values from 0 to 7, each once
- species_expert: int32 [8, 8192, 1], P('dp', 'expert'), may hold values from 0 to 63; in each aligned block of 128 rows (0 to 127, 128 to 255, ..., all dimensions but the last counted through in order) at most 4 rows name the same one
- norm_gain: float32 [2048], replicated, may hold values from 0.1 to 1.9
- expert_gate: bfloat16 [64, 2048, 704], P('expert'), may hold values from -0.125 to 0.125
- expert_up: bfloat16 [64, 2048, 704], P('expert'), may hold values from -0.125 to 0.125
- expert_down: bfloat16 [64, 704, 2048], P('expert'), may hold values from -0.21875 to 0.21875
Outputs:
- layer_out: bfloat16 [8, 8192, 2048], P('dp', 'expert')
The draws below stay inside these ranges and needn't reach their ends.
Inputs may be any that keep to these rules, and one draw needn't show every extreme that they name: `contig_lengths`: row r holds 64 contigs laid end to end from position 0, with lengths summing to 8192; the first contig of each row is shorter than 128 and the second has exactly 256 positions. Row r of the input is output slot row_target[r]; each slot is taken once. `species_expert`: among the 128 positions of an output slot held by one index of expert, no expert is named more than 4 times.
All inputs are finite; a program needn't handle non-finite values.
Results may differ from the reference program's by a relative error of at most 0.0079.
Values may be sent and summed in bfloat16 or wider, within the bound.
No kernel may reach another device: no remote copies, remote signals or barrier semaphores. Data moves between devices by JAX's collectives and lax.ppermute only.
A program may use at most 128 MiB of HBM per device.

```python
import math
import jax
import jax.numpy as jnp
import numpy as np
from jax import lax

HEADS = 16
HDIM = 128
D = 2048
HID = 704
TOK_DEV = 128
EXPERTS = 64
ROWS = 8
ROW_LEN = 8192
NSEG = 64
CMAX = 256
CAP = 4
N_EXPERT = 64


def draw_queries(key, part):
    key = jax.random.fold_in(key, 11)
    return jnp.clip(jax.random.normal(key, (ROWS, ROW_LEN, D)), -4.5, 4.5).astype(jnp.bfloat16)


def draw_key_rows(key, part):
    key = jax.random.fold_in(key, 12)
    return jnp.clip(jax.random.normal(key, (ROWS, ROW_LEN, D)), -4.5, 4.5).astype(jnp.bfloat16)


def draw_contig_lengths(key, part):
    key = jax.random.fold_in(key, 21)
    first_key, offset_key, order_key = jax.random.split(key, 3)
    first = jax.random.randint(first_key, (ROWS, 1), 1, TOK_DEV).astype(jnp.int32)
    offsets = jax.random.randint(offset_key, (ROWS, (NSEG - 4) // 2), -(TOK_DEV - 1), TOK_DEV).astype(jnp.int32)
    paired = jnp.concatenate([TOK_DEV + offsets, TOK_DEV - offsets, jnp.full((ROWS, 1), TOK_DEV, jnp.int32)], axis=1)
    shuffled = jax.random.permutation(order_key, paired, axis=1, independent=True)
    longest = jnp.full((ROWS, 1), CMAX, jnp.int32)
    return jnp.concatenate([first, longest, TOK_DEV - first, shuffled], axis=1).astype(jnp.int32)


def steps_of(stream_key, extent, pieces, smallest, top_value):
    def one(axis_at, parts):
        draws = jax.random.uniform(jax.random.fold_in(jax.random.fold_in(stream_key, 6), axis_at), (parts,), jnp.float32, smallest / len(pieces), top_value / len(pieces))
        return jnp.repeat(jnp.exp(draws), extent[axis_at] // parts).reshape((-1,) + (1,) * (len(extent) - axis_at - 1))

    loudness = one(*pieces[0])
    for cut in pieces[1:]:
        loudness = loudness * one(*cut)
    return loudness


def routed_block(rng, own, number, rows, count, top, bound, skew):
    ranking = jax.random.permutation(rng, count)
    crowded, usual = load_shares(count, rows * top, bound, skew, True), load_shares(count, rows * top, bound, skew, False)
    places = jnp.arange(count)

    def named(tallies, offset_by):
        used = int((tallies > 0).sum())
        fixed = max(1, used // 4)
        shifted = fixed + (places - fixed + offset_by * (used - fixed)) % max(1, count - fixed)
        return jnp.zeros((count,), jnp.int32).at[ranking[jnp.where(places < fixed, places, shifted)]].set(jnp.asarray(tallies, jnp.int32))

    tallies = jnp.where(number % 4 == 0, named(crowded, number // 4), named(usual, number - number // 4 - 1))
    mixed = jax.random.permutation(jax.random.fold_in(own, 3), count)
    donor, sink = mixed[0:count // 2 * 2:2], mixed[1:count // 2 * 2:2]
    room = jnp.minimum(tallies[donor] - 1, bound - tallies[sink]) // 2
    room = jnp.where((donor == ranking[0]) | (sink == ranking[0]) | (tallies[sink] == 0), 0, jnp.maximum(room, 0))
    shifted = jax.random.randint(jax.random.fold_in(own, 4), (count // 2,), 0, 1 << 20) % (room + 1)
    tallies = tallies.at[donor].add(-shifted).at[sink].add(shifted)
    items = jnp.searchsorted(jnp.cumsum(tallies), jnp.arange(rows * top), side="right").astype(jnp.int32)
    grid = items.reshape(top, rows).T
    grid = grid[jax.random.permutation(jax.random.fold_in(own, 1), rows)]
    offset_by = jax.random.randint(jax.random.fold_in(own, 2), (rows, 1), 0, top)
    return jnp.take_along_axis(grid, (jnp.arange(top)[None, :] + offset_by) % top, axis=1)


def load_shares(count, total, most, skew, full):
    loads = [(1 << 20) // math.isqrt(grade ** skew) + 1 for grade in range(1, count + 1)]
    largest = most if full else min(most, max(-(-total // count), total * loads[0] // sum(loads)))
    least = 1 if total - largest >= count - 1 else 0
    given, spare = [largest] + [least] * (count - 1), total - largest - least * (count - 1)
    while spare > 0:
        free = [i for i in range(1, count) if given[i] < largest] or [i for i in range(1, count) if given[i] < most]
        pool, remaining = sum([loads[i] for i in free]), spare
        for i in free:
            extra = min(most - given[i], max(1, remaining * loads[i] // pool), spare)
            given[i] = given[i] + extra
            spare = spare - extra
    return np.array(given)


def noise(rng, extent, spread, limit, cuts=(), held_as=jnp.bfloat16):
    array = jax.random.normal(rng, extent, jnp.float32) * spread
    if len(cuts) > 0:
        array = steps_of(rng, extent, cuts, -0.22, 0.18) * array
    return jnp.clip(array, min=-limit, max=limit).astype(held_as)


def setup_inputs(seed: int = 0) -> dict:
    streams_of = jax.random.split(jax.random.key(seed), 11)
    queries = draw_queries(jax.random.fold_in(streams_of[10], 71), 0)
    key_rows = draw_key_rows(jax.random.fold_in(streams_of[10], 71), 0)
    value_rows = noise(streams_of[2], (ROWS, ROW_LEN, D), 2.0, 8.0, ((0, 4), (1, 64)))
    contig_lengths = draw_contig_lengths(jax.random.fold_in(streams_of[10], 71), 0)
    row_target = jax.random.permutation(streams_of[4], ROWS).astype(jnp.int32)
    species_expert_keys = jax.random.split(jax.random.fold_in(streams_of[5], 1), ROWS * ROW_LEN // TOK_DEV)
    species_expert_turns = jax.random.permutation(jax.random.fold_in(streams_of[5], 3), ROWS * ROW_LEN // TOK_DEV)
    species_expert = jax.vmap(lambda own, number: routed_block(jax.random.fold_in(streams_of[5], 2), own, number, TOK_DEV, EXPERTS, 1, CAP, 2))(species_expert_keys, species_expert_turns).reshape((ROWS, ROW_LEN, 1))
    norm_gain = jnp.clip(1.0 + 0.18 * jax.random.normal(streams_of[6], (D,), jnp.float32), 0.1, 1.9)
    expert_gate = noise(streams_of[7], (EXPERTS, D, HID), D ** -0.5, 0.125, ((0, 64),))
    expert_up = noise(streams_of[8], (EXPERTS, D, HID), D ** -0.5, 0.125, ((0, 64),))
    expert_down = noise(streams_of[9], (EXPERTS, HID, D), HID ** -0.5, 0.21875, ((0, 64),))
    return {"queries": queries, "key_rows": key_rows, "value_rows": value_rows, "contig_lengths": contig_lengths, "row_target": row_target, "species_expert": species_expert, "norm_gain": norm_gain, "expert_gate": expert_gate, "expert_up": expert_up, "expert_down": expert_down}


def block_attention(query_block, key_block, value_block, query_pos, key_pos, lengths):
    contig_ends = jnp.cumsum(lengths).astype(jnp.int32)
    contig_start = lax.optimization_barrier(jnp.sum(jnp.where(contig_ends[None, :] <= query_pos[:, None], lengths[None, :], 0), axis=1)).astype(jnp.int32)
    allowed = (key_pos[None, :] >= contig_start[:, None]) & (key_pos[None, :] <= query_pos[:, None])
    query_heads = query_block.astype(jnp.float32).reshape(query_block.shape[0], HEADS, HDIM)
    key_heads = key_block.astype(jnp.float32).reshape(key_block.shape[0], HEADS, HDIM)
    value_heads = value_block.astype(jnp.float32).reshape(value_block.shape[0], HEADS, HDIM)
    scores = jnp.einsum('qhd,khd->hqk', query_heads, key_heads) / math.sqrt(HDIM)
    scores = jnp.where(allowed[None, :, :], scores, -jnp.inf)
    row_peak = lax.optimization_barrier(jnp.max(scores, axis=-1, keepdims=True))
    probabilities = jnp.exp(scores - row_peak)
    totals = lax.optimization_barrier(jnp.sum(probabilities, axis=-1))
    rounded = lax.optimization_barrier(probabilities.astype(jnp.bfloat16)).astype(jnp.float32)
    mixed_rows = jnp.einsum('hqk,khd->qhd', rounded, value_heads) / jnp.transpose(totals)[:, :, None]
    return mixed_rows.reshape(query_block.shape[0], HEADS * HDIM).astype(jnp.bfloat16)

def attend_row(query_row, key_row, value_row, lengths):
    margin = 2 * TOK_DEV
    key_padded = jnp.concatenate([jnp.zeros((margin, D), jnp.bfloat16), key_row], axis=0)
    value_padded = jnp.concatenate([jnp.zeros((margin, D), jnp.bfloat16), value_row], axis=0)

    def one_block(block_index):
        first = block_index * TOK_DEV
        query_block = lax.dynamic_slice_in_dim(query_row, first, TOK_DEV, 0)
        key_block = lax.dynamic_slice_in_dim(key_padded, first, 3 * TOK_DEV, 0)
        value_block = lax.dynamic_slice_in_dim(value_padded, first, 3 * TOK_DEV, 0)
        query_pos = (first + jnp.arange(TOK_DEV, dtype=jnp.int32)).astype(jnp.int32)
        key_pos = (first - margin + jnp.arange(3 * TOK_DEV, dtype=jnp.int32)).astype(jnp.int32)
        return block_attention(query_block, key_block, value_block, query_pos, key_pos, lengths)
    results = lax.map(one_block, jnp.arange(ROW_LEN // TOK_DEV, dtype=jnp.int32))
    return results.reshape(ROW_LEN, D)

def expert_ffn(tokens_in, gate_weight, up_weight, down_weight):
    gate_proj = jnp.dot(tokens_in, gate_weight, preferred_element_type=jnp.float32)
    up_proj = jnp.dot(tokens_in, up_weight, preferred_element_type=jnp.float32)
    activation = (jax.nn.silu(gate_proj) * up_proj).astype(jnp.bfloat16)
    return jnp.dot(activation, down_weight, preferred_element_type=jnp.float32).astype(jnp.bfloat16)

def reference(queries, key_rows, value_rows, contig_lengths, row_target, species_expert, norm_gain, expert_gate, expert_up, expert_down):
    attended = jnp.stack([attend_row(queries[row_index], key_rows[row_index], value_rows[row_index], contig_lengths[row_index]) for row_index in range(ROWS)])
    slot_range = jnp.arange(ROWS, dtype=jnp.int32)
    source = lax.optimization_barrier(jnp.sum(jnp.where(row_target[None, :] == slot_range[:, None], slot_range[None, :], 0), axis=1)).astype(jnp.int32)
    relaid = attended[source]
    hidden_f32 = relaid.astype(jnp.float32)
    mean_square = lax.optimization_barrier(jnp.mean(hidden_f32 * hidden_f32, axis=-1, keepdims=True))
    normed = (hidden_f32 * lax.rsqrt(mean_square + 1e-05) * norm_gain).astype(jnp.bfloat16)
    blocks = ROWS * N_EXPERT
    expert_ids = species_expert[:, :, 0].reshape(blocks, TOK_DEV).astype(jnp.int32)
    onehot = (expert_ids[:, :, None] == jnp.arange(EXPERTS, dtype=jnp.int32)[None, None, :]).astype(jnp.int32)
    before = (jnp.cumsum(onehot, axis=1) - onehot).astype(jnp.int32)
    position_rank = lax.optimization_barrier(jnp.sum(before * onehot, axis=-1)).astype(jnp.int32)
    block_ids = jnp.arange(blocks, dtype=jnp.int32)[:, None]
    slots = (expert_ids * (blocks * CAP) + block_ids * CAP + position_rank).reshape(-1).astype(jnp.int32)
    flat_normed = normed.reshape(-1, D)
    slot_rows = jnp.zeros((EXPERTS * blocks * CAP, D), jnp.bfloat16).at[slots].set(flat_normed)

    def run_expert(operands):
        return expert_ffn(operands[0], operands[1], operands[2], operands[3])
    produced = lax.map(run_expert, (slot_rows.reshape(EXPERTS, blocks * CAP, D), expert_gate, expert_up, expert_down))
    expert_out = produced.reshape(-1, D)[slots]
    layer_out = (hidden_f32.reshape(-1, D) + expert_out.astype(jnp.float32)).astype(jnp.bfloat16)
    return layer_out.reshape(ROWS, ROW_LEN, D)
```

```python
import functools
import itertools
import math

import jax
import jax.numpy as jnp
from jax import lax
from jax.experimental import pallas as pl
from jax.experimental.pallas import tpu as pltpu
from jax.sharding import PartitionSpec as P

HEADS = 16
HDIM = 128
CAP = 4
EXT = 128
NEG = -1e30
SCALE = math.log2(math.e) / math.sqrt(HDIM)
NT = (((1,), (1,)), ((), ()))
TN = (((0,), (0,)), ((), ()))
VMEM = pl.BlockSpec(memory_space=pltpu.VMEM)
SMEM = pl.BlockSpec(memory_space=pltpu.SMEM)
ANY = pl.BlockSpec(memory_space=pl.ANY)
MIB = 1 << 20


def params(mib):
    return pltpu.CompilerParams(vmem_limit_bytes=mib * MIB)


def cost(flops, nbytes, exps=0):
    return pl.CostEstimate(flops=flops, bytes_accessed=nbytes, transcendentals=exps)


def plan_kernel(target_ref, q_ref, plan_ref, qa_ref, qb_ref, sems):
    group = lax.axis_index("dp")
    to_group = [target_ref[r] // 2 for r in range(8)]
    weight = [jnp.left_shift(1, t) for t in to_group]
    picked = jnp.int32(-1)
    for choice in reversed(range(8)):
        bits = [0, choice & 1, (choice >> 1) & 1, (choice >> 2) & 1]
        total = sum(weight[2 * g + bits[g]] for g in range(4))
        picked = jnp.where(total == 15, choice, picked)
    picked = jnp.maximum(picked, 0)
    first = [jnp.int32(0), picked & 1, (picked >> 1) & 1, (picked >> 2) & 1]
    mine = jnp.int32(0)
    for g in range(4):
        mine = jnp.where(group == g, first[g], mine)
    copies = [
        pltpu.make_async_copy(q_ref.at[mine], qa_ref.at[0], sems.at[0]),
        pltpu.make_async_copy(q_ref.at[1 - mine], qb_ref.at[0], sems.at[1]),
    ]
    for copy in copies:
        copy.start()
    given = [
        [jnp.where(first[g] == 0, to_group[2 * g], to_group[2 * g + 1]) for g in range(4)],
        [jnp.where(first[g] == 0, to_group[2 * g + 1], to_group[2 * g]) for g in range(4)],
    ]
    slot = jnp.int32(0)
    for g in range(4):
        row_slot = jnp.where(first[g] == 0, target_ref[2 * g], target_ref[2 * g + 1]) % 2
        slot = jnp.where(given[0][g] == group, row_slot, slot)
    plan_ref[0] = mine
    for k in range(2):
        p = given[k]
        second = p[1] - (p[1] > p[0]).astype(jnp.int32)
        plan_ref[1 + k] = 6 * p[0] + 2 * second + (p[2] > p[3]).astype(jnp.int32)
    plan_ref[3] = slot
    for i in range(4, 8):
        plan_ref[i] = 0
    for copy in copies:
        copy.wait()


def make_plan(row_target, queries):
    _, width, features = queries.shape
    row = jax.ShapeDtypeStruct((1, width, features), queries.dtype)
    return pl.pallas_call(
        plan_kernel,
        out_shape=[jax.ShapeDtypeStruct((8,), jnp.int32), row, row],
        in_specs=[SMEM, ANY],
        out_specs=[SMEM, ANY, ANY],
        scratch_shapes=[pltpu.SemaphoreType.DMA((2,))],
        cost_estimate=cost(0, 4 * width * features * 2),
    )(row_target, queries)


def contig_start_of(lengths, query_pos):
    n = lengths.shape[1]
    above = lax.broadcasted_iota(jnp.int32, (n, n), 0)
    along = lax.broadcasted_iota(jnp.int32, (n, n), 1)
    spread = jnp.broadcast_to(lengths, (n, n))
    column = jnp.sum(jnp.where(above == along, spread, 0), axis=1, keepdims=True)
    ends = jnp.sum(jnp.where(above <= along, jnp.broadcast_to(column, (n, n)), 0), axis=0, keepdims=True)
    return jnp.sum(jnp.where(ends <= query_pos, lengths, 0), axis=1, keepdims=True)


def attend(lengths, q, ko, kp, vo, vp, ahead, rounded_peak, write):
    width = q.shape[0]
    shard = lax.axis_index("expert")
    first = (shard + ahead) * width
    start = contig_start_of(lengths, first + lax.broadcasted_iota(jnp.int32, (width, 1), 0))
    query_pos = first + lax.broadcasted_iota(jnp.int32, (width, width), 0)
    lane = lax.broadcasted_iota(jnp.int32, (width, width), 1)
    masks = []
    for block in (shard, shard + 1 - 2 * (shard % 2)):
        key_pos = block * width + lane
        masks.append((key_pos >= start) & (key_pos <= query_pos))
    peaks, totals = [], []
    for h in range(HEADS):
        cols = slice(h * HDIM, (h + 1) * HDIM)
        scores = [
            jnp.where(
                mask,
                lax.dot_general(q[:, cols], k[:, cols], NT, preferred_element_type=jnp.float32) * SCALE,
                NEG,
            )
            for mask, k in zip(masks, (ko, kp))
        ]
        peak = jnp.max(jnp.maximum(scores[0], scores[1]), axis=1, keepdims=True)
        if rounded_peak:
            peak = peak.astype(jnp.bfloat16).astype(jnp.float32)
        probs = [jnp.where(mask, jnp.exp2(s - peak), 0.0) for mask, s in zip(masks, scores)]
        totals.append(jnp.sum(probs[0] + probs[1], axis=1, keepdims=True))
        peaks.append(peak)
        sums = [
            jnp.dot(p.astype(jnp.bfloat16), v[:, cols], preferred_element_type=jnp.float32)
            for p, v in zip(probs, (vo, vp))
        ]
        write(h, sums[0] + sums[1])
    return peaks, totals


def spread_columns(columns_at, shape):
    lane = lax.broadcasted_iota(jnp.int32, shape, 1)
    out = jnp.zeros(shape, jnp.float32)
    for at, column in columns_at:
        out = jnp.where(lane == at, column, out)
    return out


def own_row(len_ref, row):
    return len_ref[pl.ds(lax.axis_index("dp") * 2 + row, 1), :]


def near_kernel(plan_ref, len_ref, q_ref, ko_ref, kp_ref, vo_ref, vp_ref, sums_ref, stats_ref):
    step = pl.program_id(0)
    row = jnp.where(step == 0, plan_ref[0], 1 - plan_ref[0])

    def write(h, sums):
        sums_ref[0, :, h * HDIM:(h + 1) * HDIM] = sums

    peaks, totals = attend(
        own_row(len_ref, row), q_ref[0], ko_ref[0], kp_ref[0], vo_ref[0], vp_ref[0], 0, False, write
    )
    columns = [(h, peaks[h]) for h in range(HEADS)] + [(HEADS + h, totals[h]) for h in range(HEADS)]
    stats_ref[0] = spread_columns(columns, stats_ref.shape[1:])


def near_attention(plan, lengths, queries, k_own, k_pair, v_own, v_pair):
    rows, width, features = queries.shape
    block = pl.BlockSpec(
        (1, width, features), lambda i, plan: (jnp.where(i == 0, plan[0], 1 - plan[0]), 0, 0)
    )
    return pl.pallas_call(
        near_kernel,
        out_shape=[
            jax.ShapeDtypeStruct((rows, width, features), jnp.float32),
            jax.ShapeDtypeStruct((rows, width, EXT), jnp.float32),
        ],
        grid_spec=pltpu.PrefetchScalarGridSpec(
            num_scalar_prefetch=1,
            grid=(rows,),
            in_specs=[pl.BlockSpec(lengths.shape, lambda i, plan: (0, 0))] + [block] * 5,
            out_specs=[
                pl.BlockSpec((1, width, features), lambda i, plan: (i, 0, 0)),
                pl.BlockSpec((1, width, EXT), lambda i, plan: (i, 0, 0)),
            ],
        ),
        compiler_params=params(24),
        cost_estimate=cost(rows * 4 * width * 2 * width * features, 7 * MIB, rows * HEADS * 2 * width * width),
    )(plan, lengths, queries, k_own, k_pair, v_own, v_pair)


def far_kernel(which, plan_ref, len_ref, q_ref, ko_ref, kp_ref, vo_ref, vp_ref, out_ref):
    row = plan_ref[0] if which == 0 else 1 - plan_ref[0]
    features = q_ref.shape[2]

    def write(h, sums):
        out_ref[0, :, h * HDIM:(h + 1) * HDIM] = sums.astype(jnp.bfloat16)

    peaks, totals = attend(
        own_row(len_ref, row), q_ref[0], ko_ref[0], kp_ref[0], vo_ref[0], vp_ref[0], 2, True, write
    )
    columns = [(h, peaks[h]) for h in range(HEADS)]
    for h in range(HEADS):
        high = totals[h].astype(jnp.bfloat16).astype(jnp.float32)
        columns += [(HEADS + h, high), (2 * HEADS + h, totals[h] - high)]
    stats = spread_columns(columns, (q_ref.shape[1], EXT))
    out_ref[0, :, features:] = stats.astype(jnp.bfloat16)


def far_attention(which, plan, lengths, q, k_own, k_pair, v_own, v_pair):
    _, width, features = q.shape
    block = pl.BlockSpec(
        (1, width, features), lambda i, plan: (plan[0] if which == 0 else 1 - plan[0], 0, 0)
    )
    return pl.pallas_call(
        functools.partial(far_kernel, which),
        out_shape=jax.ShapeDtypeStruct((1, width, features + EXT), jnp.bfloat16),
        grid_spec=pltpu.PrefetchScalarGridSpec(
            num_scalar_prefetch=1,
            grid=(1,),
            in_specs=[
                pl.BlockSpec(lengths.shape, lambda i, plan: (0, 0)),
                pl.BlockSpec((1, width, features), lambda i, plan: (0, 0, 0)),
            ]
            + [block] * 4,
            out_specs=pl.BlockSpec((1, width, features + EXT), lambda i, plan: (0, 0, 0)),
        ),
        compiler_params=params(24),
        cost_estimate=cost(4 * width * 2 * width * features, 3 * MIB, HEADS * 2 * width * width),
    )(plan, lengths, q, k_own, k_pair, v_own, v_pair)


def merge_kernel(sums_ref, stats_ref, far_ref, out_ref):
    features = out_ref.shape[2]
    stats = stats_ref[0]
    far_stats = far_ref[0, :, features:].astype(jnp.float32)
    peak, total = stats[:, :HEADS], stats[:, HEADS:2 * HEADS]
    far_peak = far_stats[:, :HEADS]
    far_total = far_stats[:, HEADS:2 * HEADS] + far_stats[:, 2 * HEADS:3 * HEADS]
    some = far_total > 0
    top = jnp.maximum(peak, jnp.where(some, far_peak, NEG))
    share = jnp.exp2(peak - top)
    far_share = jnp.where(some, jnp.exp2(far_peak - top), 0.0)
    whole = total * share + far_total * far_share
    share, far_share = share / whole, far_share / whole
    for h in range(HEADS):
        cols = slice(h * HDIM, (h + 1) * HDIM)
        mixed = sums_ref[0, :, cols] * share[:, h:h + 1]
        mixed += far_ref[0, :, cols].astype(jnp.float32) * far_share[:, h:h + 1]
        out_ref[0, :, cols] = mixed.astype(jnp.bfloat16)


def merge(which, sums, stats, far):
    _, width, features = sums.shape
    return pl.pallas_call(
        merge_kernel,
        out_shape=jax.ShapeDtypeStruct((1, width, features), jnp.bfloat16),
        grid=(1,),
        in_specs=[
            pl.BlockSpec((1, width, features), lambda i: (which, 0, 0)),
            pl.BlockSpec((1, width, EXT), lambda i: (which, 0, 0)),
            pl.BlockSpec((1, width, features + EXT), lambda i: (0, 0, 0)),
        ],
        out_specs=pl.BlockSpec((1, width, features), lambda i: (0, 0, 0)),
        compiler_params=params(16),
        cost_estimate=cost(4 * width * features, 2 * MIB),
    )(sums, stats, far)


def move_row(index, value):
    count = lax.axis_size("dp")
    branches = [
        functools.partial(lax.ppermute, axis_name="dp", perm=list(enumerate(perm)))
        for perm in itertools.permutations(range(count))
    ]
    return lax.switch(index, branches, value)


def around(value, steps):
    count = lax.axis_size("expert")
    return lax.ppermute(value, "expert", [(i, (i + steps) % count) for i in range(count)])


def other_core(value):
    count = lax.axis_size("expert")
    return lax.ppermute(value, "expert", [(i, i ^ 1) for i in range(count)])


def slots_of(ids, round_index):
    w = ids.shape[1]
    above = lax.broadcasted_iota(jnp.int32, (w, w), 0)
    along = lax.broadcasted_iota(jnp.int32, (w, w), 1)
    spread = jnp.broadcast_to(ids, (w, w))
    column = jnp.sum(jnp.where(above == along, spread, 0), axis=1, keepdims=True)
    rank = jnp.sum(jnp.where((column == spread) & (above < along), 1, 0), axis=0, keepdims=True)
    return ids * (2 * CAP) + round_index * CAP + rank


def all_slots(plan_ref, ids_ref):
    slot = plan_ref[3]
    return [slots_of(ids_ref[pl.ds(row, 1), :], k) for k, row in enumerate((slot, 1 - slot))]


def pack_kernel(plan_ref, ids_ref, gain_ref, a_ref, b_ref, out_ref, normed_ref):
    width, features = a_ref.shape[1:]
    gain = gain_ref[...]
    for k, ref in enumerate((a_ref, b_ref)):
        hidden = ref[0].astype(jnp.float32)
        mean_square = jnp.sum(hidden * hidden, axis=1, keepdims=True) * (1.0 / features)
        normed = hidden * lax.rsqrt(mean_square + 1e-05) * gain
        normed_ref[k * width:(k + 1) * width, :] = normed.astype(jnp.bfloat16)
    slots = jnp.concatenate(all_slots(plan_ref, ids_ref), axis=1)
    count = out_ref.shape[0]
    table = (lax.broadcasted_iota(jnp.int32, (count, 2 * width), 0) == slots).astype(jnp.float32)
    table = table.astype(jnp.bfloat16)
    for c in range(0, features, 512):
        out_ref[:, c:c + 512] = jnp.dot(
            table, normed_ref[:, c:c + 512], preferred_element_type=jnp.float32
        ).astype(jnp.bfloat16)


def pack(plan, ids, gain, a, b, count):
    _, width, features = a.shape
    return pl.pallas_call(
        pack_kernel,
        out_shape=jax.ShapeDtypeStruct((count, features), jnp.bfloat16),
        in_specs=[SMEM, VMEM, VMEM, VMEM, VMEM],
        out_specs=VMEM,
        scratch_shapes=[pltpu.VMEM((2 * width, features), jnp.bfloat16)],
        compiler_params=params(20),
        cost_estimate=cost(4 * count * width * features, 3 * MIB),
    )(plan, ids, gain, a, b)


def ffn_kernel(x_ref, gate_ref, up_ref, down_ref, out_ref, act_ref):
    hidden, features = down_ref.shape
    x = x_ref[...]
    for c in range(0, hidden, 256):
        rows = slice(c, min(c + 256, hidden))
        gate = lax.dot_general(x, gate_ref[rows, :], NT, preferred_element_type=jnp.float32)
        up = lax.dot_general(x, up_ref[rows, :], NT, preferred_element_type=jnp.float32)
        act_ref[:, rows] = (gate / (1.0 + jnp.exp(-gate)) * up).astype(jnp.bfloat16)
    act = act_ref[...]
    for c in range(0, features, 512):
        out_ref[:, c:c + 512] = jnp.dot(
            act, down_ref[:, c:c + 512], preferred_element_type=jnp.float32
        ).astype(jnp.bfloat16)


def ffn(x, gate, up, down):
    count, features = x.shape
    hidden = down.shape[0]
    return pl.pallas_call(
        ffn_kernel,
        out_shape=jax.ShapeDtypeStruct((count, features), jnp.bfloat16),
        in_specs=[VMEM] * 4,
        out_specs=VMEM,
        scratch_shapes=[pltpu.VMEM((count, hidden), jnp.bfloat16)],
        compiler_params=params(30),
        cost_estimate=cost(6 * count * hidden * features, 12 * MIB, count * hidden),
    )(x, gate, up, down)


def combine_kernel(plan_ref, ids_ref, a_ref, b_ref, got_ref, out_ref):
    width, features = a_ref.shape[1:]
    count = got_ref.shape[0]
    slot = plan_ref[3]
    slots = all_slots(plan_ref, ids_ref)
    tables = [
        (lax.broadcasted_iota(jnp.int32, (count, width), 0) == s).astype(jnp.float32).astype(jnp.bfloat16)
        for s in slots
    ]
    table = jnp.concatenate(tables, axis=1)
    for c in range(0, features, 512):
        cols = slice(c, c + 512)
        chosen = lax.dot_general(table, got_ref[:, cols], TN, preferred_element_type=jnp.float32)
        for k, (ref, place) in enumerate(((a_ref, slot), (b_ref, 1 - slot))):
            total = ref[0, :, cols].astype(jnp.float32) + chosen[k * width:(k + 1) * width]
            out_ref[place, :, cols] = total.astype(jnp.bfloat16)


def combine(plan, ids, a, b, got):
    _, width, features = a.shape
    return pl.pallas_call(
        combine_kernel,
        out_shape=jax.ShapeDtypeStruct((2, width, features), jnp.bfloat16),
        in_specs=[SMEM, VMEM, VMEM, VMEM, VMEM],
        out_specs=VMEM,
        compiler_params=params(20),
        cost_estimate=cost(4 * got.shape[0] * width * features, 4 * MIB),
    )(plan, ids, a, b, got)


def on_device(
    queries,
    key_rows,
    value_rows,
    contig_lengths,
    row_target,
    species_expert,
    norm_gain,
    expert_gate,
    expert_up,
    expert_down,
):
    rows, width, features = queries.shape
    experts = expert_gate.shape[0] * lax.axis_size("expert")
    ids = species_expert.reshape(rows, width)

    plan, q_a, q_b = make_plan(row_target, queries)
    far_q = [around(q_a, -2), around(q_b, -2)]
    k_pair, v_pair = other_core(key_rows), other_core(value_rows)
    sums, stats = near_attention(plan, contig_lengths, queries, key_rows, k_pair, value_rows, v_pair)
    far = [
        far_attention(k, plan, contig_lengths, far_q[k], key_rows, k_pair, value_rows, v_pair)
        for k in range(2)
    ]
    back = [around(f, 2) for f in far]
    moved = [move_row(plan[1 + k], merge(k, sums, stats, back[k])) for k in range(2)]

    outgoing = pack(plan, ids, norm_gain.reshape(1, features), moved[0], moved[1], experts * rows * CAP)
    arrived = lax.all_to_all(
        outgoing.reshape(experts, rows * CAP, features), "expert", split_axis=0, concat_axis=0, tiled=True
    )
    produced = ffn(
        arrived.reshape(-1, features),
        jnp.swapaxes(expert_gate, 1, 2)[0],
        jnp.swapaxes(expert_up, 1, 2)[0],
        expert_down[0],
    )
    returned = lax.all_to_all(
        produced.reshape(experts, rows * CAP, features), "expert", split_axis=0, concat_axis=0, tiled=True
    )
    return combine(plan, ids, moved[0], moved[1], returned.reshape(-1, features))


def solution(mesh):
    in_specs = (
        P("dp", "expert", None),
        P("dp", "expert", None),
        P("dp", "expert", None),
        P(),
        P(),
        P("dp", "expert", None),
        P(),
        P("expert", None, None),
        P("expert", None, None),
        P("expert", None, None),
    )
    return jax.shard_map(
        on_device,
        mesh=mesh,
        in_specs=in_specs,
        out_specs=P("dp", "expert", None),
        check_vma=False,
    )
```

```python
import functools
import itertools
import math

import jax
import jax.numpy as jnp
from jax import lax
from jax.experimental import pallas as pl
from jax.experimental.pallas import tpu as pltpu
from jax.sharding import PartitionSpec as P

HEADS = 16
HDIM = 128
CAP = 4
EXT = 128
PIECES = 2
NEG = -1e30
SCALE = math.log2(math.e) / math.sqrt(HDIM)
NT = (((1,), (1,)), ((), ()))
VMEM = pl.BlockSpec(memory_space=pltpu.VMEM)
SMEM = pl.BlockSpec(memory_space=pltpu.SMEM)
ANY = pl.BlockSpec(memory_space=pl.ANY)
MIB = 1 << 20


def params(mib):
    return pltpu.CompilerParams(vmem_limit_bytes=mib * MIB)


def cost(flops, nbytes, exps=0):
    return pl.CostEstimate(flops=flops, bytes_accessed=nbytes, transcendentals=exps)


def plan_kernel(target_ref, q_ref, plan_ref, *piece_refs):
    group = lax.axis_index("dp")
    to_group = [target_ref[r] // 2 for r in range(8)]
    weight = [jnp.left_shift(1, t) for t in to_group]
    picked = jnp.int32(-1)
    for choice in reversed(range(8)):
        bits = [0, choice & 1, (choice >> 1) & 1, (choice >> 2) & 1]
        total = sum(weight[2 * g + bits[g]] for g in range(4))
        picked = jnp.where(total == 15, choice, picked)
    picked = jnp.maximum(picked, 0)
    first = [jnp.int32(0), picked & 1, (picked >> 1) & 1, (picked >> 2) & 1]
    mine = jnp.int32(0)
    for g in range(4):
        mine = jnp.where(group == g, first[g], mine)
    for i, ref in enumerate(piece_refs):
        row = mine if i < PIECES else 1 - mine
        step = ref.shape[1]
        ref[...] = q_ref[row, :, (i % PIECES) * step:(i % PIECES + 1) * step]
    given = [
        [jnp.where(first[g] == 0, to_group[2 * g], to_group[2 * g + 1]) for g in range(4)],
        [jnp.where(first[g] == 0, to_group[2 * g + 1], to_group[2 * g]) for g in range(4)],
    ]
    slot = jnp.int32(0)
    for g in range(4):
        row_slot = jnp.where(first[g] == 0, target_ref[2 * g], target_ref[2 * g + 1]) % 2
        slot = jnp.where(given[0][g] == group, row_slot, slot)
    plan_ref[0] = mine
    for k in range(2):
        p = given[k]
        second = p[1] - (p[1] > p[0]).astype(jnp.int32)
        plan_ref[1 + k] = 6 * p[0] + 2 * second + (p[2] > p[3]).astype(jnp.int32)
    plan_ref[3] = slot
    for i in range(4, 8):
        plan_ref[i] = 0


def make_plan(row_target, queries):
    _, width, features = queries.shape
    piece = jax.ShapeDtypeStruct((width, features // PIECES), queries.dtype)
    return pl.pallas_call(
        plan_kernel,
        out_shape=[jax.ShapeDtypeStruct((8,), jnp.int32)] + [piece] * (2 * PIECES),
        in_specs=[SMEM, VMEM],
        out_specs=[SMEM] + [VMEM] * (2 * PIECES),
        compiler_params=params(8),
        cost_estimate=cost(0, 4 * width * features * 2),
    )(row_target, queries)


def contig_start_of(lengths, query_pos):
    n = lengths.shape[1]
    above = lax.broadcasted_iota(jnp.int32, (n, n), 0)
    along = lax.broadcasted_iota(jnp.int32, (n, n), 1)
    spread = jnp.broadcast_to(lengths, (n, n))
    column = jnp.sum(jnp.where(above == along, spread, 0), axis=1, keepdims=True)
    ends = jnp.sum(jnp.where(above <= along, jnp.broadcast_to(column, (n, n)), 0), axis=0, keepdims=True)
    return jnp.sum(jnp.where(ends <= query_pos, lengths, 0), axis=1, keepdims=True)


def attend(lengths, q_ref, k_ref, v_ref, ahead, rounded_peak, write):
    width = q_ref.shape[0]
    shard = lax.axis_index("expert")
    first = (shard + ahead) * width
    start = contig_start_of(lengths, first + lax.broadcasted_iota(jnp.int32, (width, 1), 0))
    query_pos = first + lax.broadcasted_iota(jnp.int32, (width, 2 * width), 0)
    lane = lax.broadcasted_iota(jnp.int32, (width, 2 * width), 1)
    pair = shard + 1 - 2 * (shard % 2)
    key_pos = jnp.where(lane < width, shard * width + lane, (pair - 1) * width + lane)
    bias = jnp.where((key_pos >= start) & (key_pos <= query_pos), 0.0, NEG)
    peaks, totals = [], []
    for h in range(q_ref.shape[1] // HDIM):
        cols = slice(h * HDIM, (h + 1) * HDIM)
        scores = lax.dot_general(q_ref[:, cols], k_ref[:, cols], NT, preferred_element_type=jnp.float32)
        scores = scores * SCALE + bias
        peak = jnp.maximum(jnp.max(scores, axis=1, keepdims=True), NEG * 0.1)
        if rounded_peak:
            peak = peak.astype(jnp.bfloat16).astype(jnp.float32)
        probs = jnp.exp2(scores - peak)
        totals.append(jnp.sum(probs, axis=1, keepdims=True))
        peaks.append(peak)
        write(h, jnp.dot(probs.astype(jnp.bfloat16), v_ref[:, cols], preferred_element_type=jnp.float32))
    return peaks, totals


def spread_columns(columns_at, shape):
    lane = lax.broadcasted_iota(jnp.int32, shape, 1)
    out = jnp.zeros(shape, jnp.float32)
    for at, column in columns_at:
        out = jnp.where(lane == at, column, out)
    return out


def own_row(len_ref, row):
    return len_ref[pl.ds(lax.axis_index("dp") * 2 + row, 1), :]


def near_kernel(
    which, plan_ref, len_ref, ko_ref, kp_ref, vo_ref, vp_ref, *refs
):
    q_refs, (sums_ref, stats_ref, k_ref, v_ref) = refs[:PIECES], refs[PIECES:]
    row = plan_ref[0] if which == 0 else 1 - plan_ref[0]
    width, step = q_refs[0].shape
    for both, own, pair in ((k_ref, ko_ref, kp_ref), (v_ref, vo_ref, vp_ref)):
        both[:width, :] = own[row]
        both[width:, :] = pair[row]
    columns = []
    for i, q_ref in enumerate(q_refs):
        cols = slice(i * step, (i + 1) * step)

        def write(h, sums):
            sums_ref[:, i * step + h * HDIM:i * step + (h + 1) * HDIM] = sums

        peaks, totals = attend(
            own_row(len_ref, row), q_ref, k_ref.at[:, cols], v_ref.at[:, cols], 0, False, write
        )
        for h, (peak, total) in enumerate(zip(peaks, totals)):
            at = i * len(peaks) + h
            columns += [(at, peak), (HEADS + at, total)]
    stats_ref[...] = spread_columns(columns, stats_ref.shape)


def near_attention(which, plan, lengths, pieces, k_own, k_pair, v_own, v_pair):
    _, width, features = k_own.shape
    both = jax.ShapeDtypeStruct((2 * width, features), k_own.dtype)
    return pl.pallas_call(
        functools.partial(near_kernel, which),
        out_shape=[
            jax.ShapeDtypeStruct((width, features), jnp.float32),
            jax.ShapeDtypeStruct((width, EXT), jnp.float32),
            both,
            both,
        ],
        in_specs=[SMEM] + [VMEM] * (5 + PIECES),
        out_specs=[VMEM] * 4,
        compiler_params=params(20),
        cost_estimate=cost(4 * width * 2 * width * features, 6 * MIB, HEADS * 2 * width * width),
    )(plan, lengths, k_own, k_pair, v_own, v_pair, *pieces)


def far_kernel(which, index, plan_ref, len_ref, q_ref, k_ref, v_ref, out_ref):
    row = plan_ref[0] if which == 0 else 1 - plan_ref[0]
    width, step = q_ref.shape
    cols = slice(index * step, (index + 1) * step)

    def write(h, sums):
        out_ref[:, h * HDIM:(h + 1) * HDIM] = sums.astype(jnp.bfloat16)

    peaks, totals = attend(
        own_row(len_ref, row), q_ref, k_ref.at[:, cols], v_ref.at[:, cols], 2, True, write
    )
    columns = []
    for h, (peak, total) in enumerate(zip(peaks, totals)):
        high = total.astype(jnp.bfloat16).astype(jnp.float32)
        columns += [(h, peak), (HEADS + h, high), (2 * HEADS + h, total - high)]
    out_ref[:, step:] = spread_columns(columns, (width, EXT)).astype(jnp.bfloat16)


def far_attention(which, index, plan, lengths, q, k, v):
    width, step = q.shape
    return pl.pallas_call(
        functools.partial(far_kernel, which, index),
        out_shape=jax.ShapeDtypeStruct((width, step + EXT), jnp.bfloat16),
        in_specs=[SMEM, VMEM, VMEM, VMEM, VMEM],
        out_specs=VMEM,
        compiler_params=params(12),
        cost_estimate=cost(4 * width * 2 * width * step, 3 * MIB, step // HDIM * 2 * width * width),
    )(plan, lengths, q, k, v)


def merge_kernel(sums_ref, stats_ref, *refs):
    far_refs, out_ref = refs[:PIECES], refs[PIECES]
    step = far_refs[0].shape[1] - EXT
    count = step // HDIM
    for i, far_ref in enumerate(far_refs):
        first = i * count
        peak = stats_ref[:, first:first + count]
        total = stats_ref[:, HEADS + first:HEADS + first + count]
        far_stats = far_ref[:, step:].astype(jnp.float32)
        far_peak = far_stats[:, :count]
        far_total = far_stats[:, HEADS:HEADS + count] + far_stats[:, 2 * HEADS:2 * HEADS + count]
        some = far_total > 0
        top = jnp.maximum(peak, jnp.where(some, far_peak, NEG))
        share = jnp.exp2(peak - top)
        far_share = jnp.where(some, jnp.exp2(far_peak - top), 0.0)
        whole = total * share + far_total * far_share
        share, far_share = share / whole, far_share / whole
        for h in range(count):
            cols = slice(i * step + h * HDIM, i * step + (h + 1) * HDIM)
            mixed = sums_ref[:, cols] * share[:, h:h + 1]
            mixed += far_ref[:, h * HDIM:(h + 1) * HDIM].astype(jnp.float32) * far_share[:, h:h + 1]
            out_ref[:, cols] = mixed.astype(jnp.bfloat16)


def merge(sums, stats, far):
    width, features = sums.shape
    return pl.pallas_call(
        merge_kernel,
        out_shape=jax.ShapeDtypeStruct((width, features), jnp.bfloat16),
        in_specs=[VMEM] * (2 + PIECES),
        out_specs=VMEM,
        compiler_params=params(8),
        cost_estimate=cost(4 * width * features, 2 * MIB),
    )(sums, stats, *far)


def move_row(index, value):
    count = lax.axis_size("dp")
    branches = [
        functools.partial(lax.ppermute, axis_name="dp", perm=list(enumerate(perm)))
        for perm in itertools.permutations(range(count))
    ]
    return lax.switch(index, branches, value)


def around(value, steps):
    count = lax.axis_size("expert")
    return lax.ppermute(value, "expert", [(i, (i + steps) % count) for i in range(count)])


def other_core(value):
    count = lax.axis_size("expert")
    return lax.ppermute(value, "expert", [(i, i ^ 1) for i in range(count)])


def slots_of(ids, round_index):
    w = ids.shape[1]
    above = lax.broadcasted_iota(jnp.int32, (w, w), 0)
    along = lax.broadcasted_iota(jnp.int32, (w, w), 1)
    spread = jnp.broadcast_to(ids, (w, w))
    column = jnp.sum(jnp.where(above == along, spread, 0), axis=1, keepdims=True)
    rank = jnp.sum(jnp.where((column == spread) & (above < along), 1, 0), axis=0, keepdims=True)
    return ids * (2 * CAP) + round_index * CAP + rank


def all_slots(plan_ref, ids_ref):
    slot = plan_ref[3]
    return [slots_of(ids_ref[pl.ds(row, 1), :], k) for k, row in enumerate((slot, 1 - slot))]


def pack_kernel(plan_ref, ids_ref, gain_ref, a_hbm, b_hbm, out_ref, kept_ref, normed_ref, sems):
    width, features = a_hbm.shape
    copies = [
        pltpu.make_async_copy(hbm, kept_ref.at[k * width:(k + 1) * width], sems.at[k])
        for k, hbm in enumerate((a_hbm, b_hbm))
    ]
    for copy in copies:
        copy.start()
    slots = jnp.concatenate(all_slots(plan_ref, ids_ref), axis=1)
    count = out_ref.shape[0]
    table = (lax.broadcasted_iota(jnp.int32, (count, 2 * width), 0) == slots).astype(jnp.float32)
    table = table.astype(jnp.bfloat16)
    gain = gain_ref[...]
    for k, copy in enumerate(copies):
        copy.wait()
        rows = slice(k * width, (k + 1) * width)
        hidden = kept_ref[rows, :].astype(jnp.float32)
        mean_square = jnp.sum(hidden * hidden, axis=1, keepdims=True) * (1.0 / features)
        normed = hidden * lax.rsqrt(mean_square + 1e-05) * gain
        normed_ref[rows, :] = normed.astype(jnp.bfloat16)
    for c in range(0, features, 512):
        out_ref[:, c:c + 512] = jnp.dot(
            table, normed_ref[:, c:c + 512], preferred_element_type=jnp.float32
        ).astype(jnp.bfloat16)


def pack(plan, ids, gain, a, b, count):
    width, features = a.shape
    return pl.pallas_call(
        pack_kernel,
        out_shape=[
            jax.ShapeDtypeStruct((count, features), jnp.bfloat16),
            jax.ShapeDtypeStruct((2 * width, features), jnp.bfloat16),
        ],
        in_specs=[SMEM, VMEM, VMEM, ANY, ANY],
        out_specs=[VMEM, VMEM],
        scratch_shapes=[
            pltpu.VMEM((2 * width, features), jnp.bfloat16),
            pltpu.SemaphoreType.DMA((2,)),
        ],
        compiler_params=params(16),
        cost_estimate=cost(4 * count * width * features, 3 * MIB),
    )(plan, ids, gain, a, b)


def ffn_kernel(x_ref, gate_ref, up_ref, down_ref, out_ref, act_ref):
    hidden, features = down_ref.shape
    x = x_ref[...]
    for c in range(0, hidden, 256):
        rows = slice(c, min(c + 256, hidden))
        gate = lax.dot_general(x, gate_ref[rows, :], NT, preferred_element_type=jnp.float32)
        up = lax.dot_general(x, up_ref[rows, :], NT, preferred_element_type=jnp.float32)
        act_ref[:, rows] = (gate / (1.0 + jnp.exp(-gate)) * up).astype(jnp.bfloat16)
    act = act_ref[...]
    for c in range(0, features, 512):
        out_ref[:, c:c + 512] = jnp.dot(
            act, down_ref[:, c:c + 512], preferred_element_type=jnp.float32
        ).astype(jnp.bfloat16)


def ffn(x, gate, up, down):
    count, features = x.shape
    hidden = down.shape[0]
    return pl.pallas_call(
        ffn_kernel,
        out_shape=jax.ShapeDtypeStruct((count, features), jnp.bfloat16),
        in_specs=[VMEM] * 4,
        out_specs=VMEM,
        scratch_shapes=[pltpu.VMEM((count, hidden), jnp.bfloat16)],
        compiler_params=params(20),
        cost_estimate=cost(6 * count * hidden * features, 12 * MIB, count * hidden),
    )(x, gate, up, down)


def combine_kernel(plan_ref, ids_ref, kept_ref, got_ref, out_hbm, out_ref, sems):
    rows, width, features = out_hbm.shape
    slot = plan_ref[3]
    above = lax.broadcasted_iota(jnp.int32, (width, width), 0)
    along = lax.broadcasted_iota(jnp.int32, (width, width), 1)
    place = lax.broadcasted_iota(jnp.int32, (width, got_ref.shape[0]), 1)
    tables = []
    for slots in all_slots(plan_ref, ids_ref):
        column = jnp.sum(jnp.where(above == along, slots, 0), axis=1, keepdims=True)
        tables.append((place == column).astype(jnp.float32).astype(jnp.bfloat16))
    table = jnp.concatenate(tables, axis=0)
    copies = []
    for i, c in enumerate(range(0, features, 512)):
        cols = slice(c, c + 512)
        chosen = jnp.dot(table, got_ref[:, cols], preferred_element_type=jnp.float32)
        total = (kept_ref[:, cols].astype(jnp.float32) + chosen).astype(jnp.bfloat16)
        out_ref[slot, :, cols] = total[:width]
        out_ref[1 - slot, :, cols] = total[width:]
        copies.append(pltpu.make_async_copy(out_ref.at[:, :, cols], out_hbm.at[:, :, cols], sems.at[i]))
        copies[-1].start()
    for copy in copies:
        copy.wait()


def combine(plan, ids, kept, got, rows):
    count, features = got.shape
    width = kept.shape[0] // rows
    return pl.pallas_call(
        combine_kernel,
        out_shape=jax.ShapeDtypeStruct((rows, width, features), jnp.bfloat16),
        in_specs=[SMEM, VMEM, VMEM, VMEM],
        out_specs=ANY,
        scratch_shapes=[
            pltpu.VMEM((rows, width, features), jnp.bfloat16),
            pltpu.SemaphoreType.DMA((features // 512,)),
        ],
        compiler_params=params(16),
        cost_estimate=cost(4 * count * width * features, 4 * MIB),
    )(plan, ids, kept, got)


def on_device(
    queries,
    key_rows,
    value_rows,
    contig_lengths,
    row_target,
    species_expert,
    norm_gain,
    expert_gate,
    expert_up,
    expert_down,
):
    rows, width, features = queries.shape
    experts = expert_gate.shape[0] * lax.axis_size("expert")
    ids = species_expert.reshape(rows, width)

    plan, *pieces = make_plan(row_target, queries)
    far_q = [around(piece, -2) for piece in pieces]
    k_pair, v_pair = other_core(key_rows), other_core(value_rows)
    near = [
        near_attention(
            k, plan, contig_lengths, pieces[k * PIECES:(k + 1) * PIECES], key_rows, k_pair, value_rows, v_pair
        )
        for k in range(2)
    ]
    far_q[0], near = lax.optimization_barrier((far_q[0], near))
    far, back = [], []
    for i, q in enumerate(far_q):
        k = i // PIECES
        if i:
            q, _ = lax.optimization_barrier((q, far[-1]))
        far.append(far_attention(k, i % PIECES, plan, contig_lengths, q, *near[k][2:]))
        back.append(around(far[-1], 2))
    moved = []
    after = far[-1]
    for k in range(2):
        mine, _ = lax.optimization_barrier((back[k * PIECES:(k + 1) * PIECES], after))
        after = move_row(plan[1 + k], merge(*near[k][:2], mine))
        moved.append(after)

    outgoing, kept = pack(plan, ids, norm_gain.reshape(1, features), moved[0], moved[1], experts * rows * CAP)
    arrived = lax.all_to_all(
        outgoing.reshape(experts, rows * CAP, features), "expert", split_axis=0, concat_axis=0, tiled=True
    )
    produced = ffn(
        arrived.reshape(-1, features),
        jnp.swapaxes(expert_gate, 1, 2)[0],
        jnp.swapaxes(expert_up, 1, 2)[0],
        expert_down[0],
    )
    returned = lax.all_to_all(
        produced.reshape(experts, rows * CAP, features), "expert", split_axis=0, concat_axis=0, tiled=True
    )
    return combine(plan, ids, kept, returned.reshape(-1, features), rows)


def solution(mesh):
    in_specs = (
        P("dp", "expert", None),
        P("dp", "expert", None),
        P("dp", "expert", None),
        P(),
        P(),
        P("dp", "expert", None),
        P(),
        P("expert", None, None),
        P("expert", None, None),
        P("expert", None, None),
    )
    return jax.shard_map(
        on_device,
        mesh=mesh,
        in_specs=in_specs,
        out_specs=P("dp", "expert", None),
        check_vma=False,
    )
```

```python
import functools
import itertools
import math

import jax
import jax.numpy as jnp
from jax import lax
from jax.experimental import pallas as pl
from jax.experimental.pallas import tpu as pltpu
from jax.sharding import PartitionSpec as P

HEADS = 16
HDIM = 128
CAP = 4
EXT = 128
SPLITS = ((16,), (16,))
NEG = -1e30
SCALE = math.log2(math.e) / math.sqrt(HDIM)
NT = (((1,), (1,)), ((), ()))
VMEM = pl.BlockSpec(memory_space=pltpu.VMEM)
SMEM = pl.BlockSpec(memory_space=pltpu.SMEM)
ANY = pl.BlockSpec(memory_space=pl.ANY)
MIB = 1 << 20
PERMS = 24
PLAN_MIB = 8
FFN_MIB = 44


def params(mib):
    return pltpu.CompilerParams(vmem_limit_bytes=mib * MIB)


def cost(flops, nbytes, exps=0):
    return pl.CostEstimate(flops=flops, bytes_accessed=nbytes, transcendentals=exps)


def parts_of(splits):
    for k, heads in enumerate(splits):
        first = 0
        for count in heads:
            yield k, slice(first * HDIM, (first + count) * HDIM)
            first += count


PARTS = tuple(parts_of(SPLITS))


def of_row(values, which):
    return [value for value, (k, _) in zip(values, PARTS) if k == which]


def plan_kernel(target_ref, q_ref, plan_ref, *refs):
    piece_refs, sems = refs[:-1], refs[-1]
    group = lax.axis_index("dp")
    to_group = [target_ref[r] // 2 for r in range(8)]
    weight = [jnp.left_shift(1, t) for t in to_group]
    picked = jnp.int32(-1)
    for choice in reversed(range(8)):
        bits = [0, choice & 1, (choice >> 1) & 1, (choice >> 2) & 1]
        total = sum(weight[2 * g + bits[g]] for g in range(4))
        picked = jnp.where(total == 15, choice, picked)
    picked = jnp.maximum(picked, 0)
    first = [jnp.int32(0), picked & 1, (picked >> 1) & 1, (picked >> 2) & 1]
    mine = jnp.int32(0)
    for g in range(4):
        mine = jnp.where(group == g, first[g], mine)
    copies = []
    for i, (k, cols) in enumerate(PARTS):
        row = mine if k == 0 else 1 - mine
        copies.append(pltpu.make_async_copy(q_ref.at[row, :, cols], piece_refs[i], sems.at[i]))
        copies[-1].start()
    given = [
        [jnp.where(first[g] == 0, to_group[2 * g], to_group[2 * g + 1]) for g in range(4)],
        [jnp.where(first[g] == 0, to_group[2 * g + 1], to_group[2 * g]) for g in range(4)],
    ]
    slot = jnp.int32(0)
    for g in range(4):
        row_slot = jnp.where(first[g] == 0, target_ref[2 * g], target_ref[2 * g + 1]) % 2
        slot = jnp.where(given[0][g] == group, row_slot, slot)
    plan_ref[0] = mine
    for k in range(2):
        p = given[k]
        second = p[1] - (p[1] > p[0]).astype(jnp.int32)
        plan_ref[1 + k] = 6 * p[0] + 2 * second + (p[2] > p[3]).astype(jnp.int32)
    plan_ref[3] = slot
    for i in range(4, 8):
        plan_ref[i] = 0
    for copy in copies:
        copy.wait()


def make_plan(row_target, queries):
    _, width, _ = queries.shape
    pieces = [jax.ShapeDtypeStruct((width, c.stop - c.start), queries.dtype) for _, c in PARTS]
    return pl.pallas_call(
        plan_kernel,
        out_shape=[jax.ShapeDtypeStruct((8,), jnp.int32)] + pieces,
        in_specs=[SMEM, ANY],
        out_specs=[SMEM] + [VMEM] * len(pieces),
        scratch_shapes=[pltpu.SemaphoreType.DMA((len(pieces),))],
        compiler_params=params(PLAN_MIB),
        cost_estimate=cost(0, 4 * MIB),
    )(row_target, queries)


def contig_start_of(lengths, query_pos):
    n = lengths.shape[1]
    above = lax.broadcasted_iota(jnp.int32, (n, n), 0)
    along = lax.broadcasted_iota(jnp.int32, (n, n), 1)
    spread = jnp.broadcast_to(lengths, (n, n))
    column = jnp.sum(jnp.where(above == along, spread, 0), axis=1, keepdims=True)
    ends = jnp.sum(jnp.where(above <= along, jnp.broadcast_to(column, (n, n)), 0), axis=0, keepdims=True)
    return jnp.sum(jnp.where(ends <= query_pos, lengths, 0), axis=1, keepdims=True)


def attend(lengths, q_ref, k_ref, v_ref, ahead, rounded_peak, write):
    width = q_ref.shape[0]
    shard = lax.axis_index("expert")
    first = (shard + ahead) * width
    start = contig_start_of(lengths, first + lax.broadcasted_iota(jnp.int32, (width, 1), 0))
    query_pos = first + lax.broadcasted_iota(jnp.int32, (width, 2 * width), 0)
    lane = lax.broadcasted_iota(jnp.int32, (width, 2 * width), 1)
    pair = shard + 1 - 2 * (shard % 2)
    key_pos = jnp.where(lane < width, shard * width + lane, (pair - 1) * width + lane)
    bias = jnp.where((key_pos >= start) & (key_pos <= query_pos), 0.0, NEG)
    peaks, totals = [], []
    for h in range(q_ref.shape[1] // HDIM):
        cols = slice(h * HDIM, (h + 1) * HDIM)
        scores = lax.dot_general(q_ref[:, cols], k_ref[:, cols], NT, preferred_element_type=jnp.float32)
        scores = scores * SCALE + bias
        peak = jnp.maximum(jnp.max(scores, axis=1, keepdims=True), NEG * 0.1)
        if rounded_peak:
            peak = peak.astype(jnp.bfloat16).astype(jnp.float32)
        probs = jnp.exp2(scores - peak)
        totals.append(jnp.sum(probs, axis=1, keepdims=True))
        peaks.append(peak)
        write(h, jnp.dot(probs.astype(jnp.bfloat16), v_ref[:, cols], preferred_element_type=jnp.float32))
    return peaks, totals


def spread_columns(columns_at, shape):
    lane = lax.broadcasted_iota(jnp.int32, shape, 1)
    out = jnp.zeros(shape, jnp.float32)
    for at, column in columns_at:
        out = jnp.where(lane == at, column, out)
    return out


def own_row(len_ref, row):
    return len_ref[pl.ds(lax.axis_index("dp") * 2 + row, 1), :]


def near_kernel(
    which, plan_ref, len_ref, ko_ref, kp_ref, vo_ref, vp_ref, *refs
):
    q_refs, (sums_ref, stats_ref, k_ref, v_ref) = refs[:-4], refs[-4:]
    row = plan_ref[0] if which == 0 else 1 - plan_ref[0]
    width = q_refs[0].shape[0]
    for both, own, pair in ((k_ref, ko_ref, kp_ref), (v_ref, vo_ref, vp_ref)):
        both[:width, :] = own[row]
        both[width:, :] = pair[row]
    columns = []
    for q_ref, cols in zip(q_refs, [c for k, c in PARTS if k == which]):

        def write(h, sums):
            sums_ref[:, cols.start + h * HDIM:cols.start + (h + 1) * HDIM] = sums

        peaks, totals = attend(
            own_row(len_ref, row), q_ref, k_ref.at[:, cols], v_ref.at[:, cols], 0, False, write
        )
        for h, (peak, total) in enumerate(zip(peaks, totals)):
            at = cols.start // HDIM + h
            columns += [(at, peak), (HEADS + at, total)]
    stats_ref[...] = spread_columns(columns, stats_ref.shape)


def near_attention(which, plan, lengths, pieces, k_own, k_pair, v_own, v_pair):
    _, width, features = k_own.shape
    both = jax.ShapeDtypeStruct((2 * width, features), k_own.dtype)
    return pl.pallas_call(
        functools.partial(near_kernel, which),
        out_shape=[
            jax.ShapeDtypeStruct((width, features), jnp.float32),
            jax.ShapeDtypeStruct((width, EXT), jnp.float32),
            both,
            both,
        ],
        in_specs=[SMEM] + [VMEM] * (4 + 1 + len(pieces)),
        out_specs=[VMEM] * 4,
        compiler_params=params(20),
        cost_estimate=cost(4 * width * 2 * width * features, 6 * MIB, HEADS * 2 * width * width),
    )(plan, lengths, k_own, k_pair, v_own, v_pair, *pieces)


def far_kernel(index, plan_ref, len_ref, q_ref, k_ref, v_ref, out_ref):
    row = plan_ref[0] if PARTS[index][0] == 0 else 1 - plan_ref[0]
    width, step = q_ref.shape
    cols = PARTS[index][1]

    def write(h, sums):
        out_ref[:, h * HDIM:(h + 1) * HDIM] = sums.astype(jnp.bfloat16)

    peaks, totals = attend(
        own_row(len_ref, row), q_ref, k_ref.at[:, cols], v_ref.at[:, cols], 2, True, write
    )
    columns = []
    for h, (peak, total) in enumerate(zip(peaks, totals)):
        high = total.astype(jnp.bfloat16).astype(jnp.float32)
        columns += [(h, peak), (HEADS + h, high), (2 * HEADS + h, total - high)]
    out_ref[:, step:] = spread_columns(columns, (width, EXT)).astype(jnp.bfloat16)


def far_attention(index, plan, lengths, q, k, v):
    width, step = q.shape
    return pl.pallas_call(
        functools.partial(far_kernel, index),
        out_shape=jax.ShapeDtypeStruct((width, step + EXT), jnp.bfloat16),
        in_specs=[SMEM, VMEM, VMEM, VMEM, VMEM],
        out_specs=VMEM,
        compiler_params=params(12),
        cost_estimate=cost(4 * width * 2 * width * step, 3 * MIB, step // HDIM * 2 * width * width),
    )(plan, lengths, q, k, v)


def merge_kernel(sums_ref, stats_ref, *refs):
    far_refs, out_ref = refs[:-1], refs[-1]
    first = 0
    for far_ref in far_refs:
        step = far_ref.shape[1] - EXT
        count = step // HDIM
        peak = stats_ref[:, first:first + count]
        total = stats_ref[:, HEADS + first:HEADS + first + count]
        far_stats = far_ref[:, step:].astype(jnp.float32)
        far_peak = far_stats[:, :count]
        far_total = far_stats[:, HEADS:HEADS + count] + far_stats[:, 2 * HEADS:2 * HEADS + count]
        some = far_total > 0
        top = jnp.maximum(peak, jnp.where(some, far_peak, NEG))
        share = jnp.exp2(peak - top)
        far_share = jnp.where(some, jnp.exp2(far_peak - top), 0.0)
        whole = total * share + far_total * far_share
        share, far_share = share / whole, far_share / whole
        for h in range(count):
            cols = slice((first + h) * HDIM, (first + h + 1) * HDIM)
            mixed = sums_ref[:, cols] * share[:, h:h + 1]
            mixed += far_ref[:, h * HDIM:(h + 1) * HDIM].astype(jnp.float32) * far_share[:, h:h + 1]
            out_ref[:, cols] = mixed.astype(jnp.bfloat16)
        first += count


def merge(sums, stats, far):
    width, features = sums.shape
    return pl.pallas_call(
        merge_kernel,
        out_shape=jax.ShapeDtypeStruct((width, features), jnp.bfloat16),
        in_specs=[VMEM] * (2 + len(far)),
        out_specs=VMEM,
        compiler_params=params(8),
        cost_estimate=cost(4 * width * features, 2 * MIB),
    )(sums, stats, *far)


def move_row(index, value):
    count = lax.axis_size("dp")
    branches = [
        functools.partial(lax.ppermute, axis_name="dp", perm=list(enumerate(perm)))
        for perm in itertools.permutations(range(count))
    ]
    return lax.switch(index, branches, value)


def around(value, steps):
    count = lax.axis_size("expert")
    return lax.ppermute(value, "expert", [(i, (i + steps) % count) for i in range(count)])


def other_core(value):
    count = lax.axis_size("expert")
    return lax.ppermute(value, "expert", [(i, i ^ 1) for i in range(count)])


def slots_of(ids, round_index):
    w = ids.shape[1]
    above = lax.broadcasted_iota(jnp.int32, (w, w), 0)
    along = lax.broadcasted_iota(jnp.int32, (w, w), 1)
    spread = jnp.broadcast_to(ids, (w, w))
    column = jnp.sum(jnp.where(above == along, spread, 0), axis=1, keepdims=True)
    rank = jnp.sum(jnp.where((column == spread) & (above < along), 1, 0), axis=0, keepdims=True)
    return ids * (2 * CAP) + round_index * CAP + rank


def all_slots(plan_ref, ids_ref):
    slot = plan_ref[3]
    return [slots_of(ids_ref[pl.ds(row, 1), :], k) for k, row in enumerate((slot, 1 - slot))]


def pack_kernel(plan_ref, ids_ref, gain_ref, a_hbm, b_hbm, out_ref, kept_ref, normed_ref, sems):
    width, features = a_hbm.shape
    copies = [
        pltpu.make_async_copy(hbm, kept_ref.at[k * width:(k + 1) * width], sems.at[k])
        for k, hbm in enumerate((a_hbm, b_hbm))
    ]
    for copy in copies:
        copy.start()
    slots = jnp.concatenate(all_slots(plan_ref, ids_ref), axis=1)
    count = out_ref.shape[0]
    table = (lax.broadcasted_iota(jnp.int32, (count, 2 * width), 0) == slots).astype(jnp.float32)
    table = table.astype(jnp.bfloat16)
    gain = gain_ref[...]
    for k, copy in enumerate(copies):
        copy.wait()
        rows = slice(k * width, (k + 1) * width)
        hidden = kept_ref[rows, :].astype(jnp.float32)
        mean_square = jnp.sum(hidden * hidden, axis=1, keepdims=True) * (1.0 / features)
        normed = hidden * lax.rsqrt(mean_square + 1e-05) * gain
        normed_ref[rows, :] = normed.astype(jnp.bfloat16)
    for c in range(0, features, 512):
        out_ref[:, c:c + 512] = jnp.dot(
            table, normed_ref[:, c:c + 512], preferred_element_type=jnp.float32
        ).astype(jnp.bfloat16)


def pack(plan, ids, gain, a, b, count):
    width, features = a.shape
    return pl.pallas_call(
        pack_kernel,
        out_shape=[
            jax.ShapeDtypeStruct((count, features), jnp.bfloat16),
            jax.ShapeDtypeStruct((2 * width, features), jnp.bfloat16),
        ],
        in_specs=[SMEM, VMEM, VMEM, ANY, ANY],
        out_specs=[VMEM, VMEM],
        scratch_shapes=[
            pltpu.VMEM((2 * width, features), jnp.bfloat16),
            pltpu.SemaphoreType.DMA((2,)),
        ],
        compiler_params=params(16),
        cost_estimate=cost(4 * count * width * features, 3 * MIB),
    )(plan, ids, gain, a, b)


def ffn_kernel(x_ref, gate_ref, up_ref, down_hbm, out_ref, act_ref, down_ref, sems):
    hidden, features = down_ref.shape
    copies = [
        pltpu.make_async_copy(down_hbm.at[:, c:c + 512], down_ref.at[:, c:c + 512], sems.at[i])
        for i, c in enumerate(range(0, features, 512))
    ]
    for copy in copies:
        copy.start()
    x = x_ref[...]
    for c in range(0, hidden, 256):
        rows = slice(c, min(c + 256, hidden))
        gate = lax.dot_general(x, gate_ref[rows, :], NT, preferred_element_type=jnp.float32)
        up = lax.dot_general(x, up_ref[rows, :], NT, preferred_element_type=jnp.float32)
        act_ref[:, rows] = (gate / (1.0 + jnp.exp(-gate)) * up).astype(jnp.bfloat16)
    act = act_ref[...]
    for copy, c in zip(copies, range(0, features, 512)):
        copy.wait()
        out_ref[:, c:c + 512] = jnp.dot(
            act, down_ref[:, c:c + 512], preferred_element_type=jnp.float32
        ).astype(jnp.bfloat16)


def ffn(x, gate, up, down):
    count, features = x.shape
    hidden = down.shape[0]
    return pl.pallas_call(
        ffn_kernel,
        out_shape=jax.ShapeDtypeStruct((count, features), jnp.bfloat16),
        in_specs=[VMEM, VMEM, VMEM, ANY],
        out_specs=VMEM,
        scratch_shapes=[
            pltpu.VMEM((count, hidden), jnp.bfloat16),
            pltpu.VMEM((hidden, features), jnp.bfloat16),
            pltpu.SemaphoreType.DMA((features // 512,)),
        ],
        compiler_params=params(FFN_MIB),
        cost_estimate=cost(6 * count * hidden * features, 12 * MIB, count * hidden),
    )(x, gate, up, down)


def combine_kernel(plan_ref, ids_ref, kept_ref, got_ref, out_hbm, out_ref, sems):
    rows, width, features = out_hbm.shape
    slot = plan_ref[3]
    above = lax.broadcasted_iota(jnp.int32, (width, width), 0)
    along = lax.broadcasted_iota(jnp.int32, (width, width), 1)
    place = lax.broadcasted_iota(jnp.int32, (width, got_ref.shape[0]), 1)
    tables = []
    for slots in all_slots(plan_ref, ids_ref):
        column = jnp.sum(jnp.where(above == along, slots, 0), axis=1, keepdims=True)
        tables.append((place == column).astype(jnp.float32).astype(jnp.bfloat16))
    table = jnp.concatenate(tables, axis=0)
    copies = []
    for i, c in enumerate(range(0, features, 512)):
        cols = slice(c, c + 512)
        chosen = jnp.dot(table, got_ref[:, cols], preferred_element_type=jnp.float32)
        total = (kept_ref[:, cols].astype(jnp.float32) + chosen).astype(jnp.bfloat16)
        out_ref[slot, :, cols] = total[:width]
        out_ref[1 - slot, :, cols] = total[width:]
        copies.append(pltpu.make_async_copy(out_ref.at[:, :, cols], out_hbm.at[:, :, cols], sems.at[i]))
        copies[-1].start()
    for copy in copies:
        copy.wait()


def combine(plan, ids, kept, got, rows):
    count, features = got.shape
    width = kept.shape[0] // rows
    return pl.pallas_call(
        combine_kernel,
        out_shape=jax.ShapeDtypeStruct((rows, width, features), jnp.bfloat16),
        in_specs=[SMEM, VMEM, VMEM, VMEM],
        out_specs=ANY,
        scratch_shapes=[
            pltpu.VMEM((rows, width, features), jnp.bfloat16),
            pltpu.SemaphoreType.DMA((features // 512,)),
        ],
        compiler_params=params(16),
        cost_estimate=cost(4 * count * width * features, 4 * MIB),
    )(plan, ids, kept, got)


def on_device(
    queries,
    key_rows,
    value_rows,
    contig_lengths,
    row_target,
    species_expert,
    norm_gain,
    expert_gate,
    expert_up,
    expert_down,
):
    rows, width, features = queries.shape
    experts = expert_gate.shape[0] * lax.axis_size("expert")
    ids = species_expert.reshape(rows, width)

    plan, *pieces = make_plan(row_target, queries)
    far_q = [around(piece, -2) for piece in pieces]
    k_pair, v_pair = other_core(key_rows), other_core(value_rows)
    near = [
        near_attention(
            k, plan, contig_lengths, of_row(pieces, k), key_rows, k_pair, value_rows, v_pair
        )
        for k in range(2)
    ]
    perms = [lax.clamp(0, plan[1 + k], PERMS - 1) for k in range(2)]
    far_q[0], near = lax.optimization_barrier((far_q[0], near))
    far_q[0], _ = lax.optimization_barrier((far_q[0], perms))
    far, back = [], []
    for i, q in enumerate(far_q):
        k = PARTS[i][0]
        if i:
            q, _ = lax.optimization_barrier((q, far[-1]))
        far.append(far_attention(i, plan, contig_lengths, q, *near[k][2:]))
        back.append(around(far[-1], 2))
    moved = []
    after = far[-1]
    for k in range(2):
        mine, _ = lax.optimization_barrier((of_row(back, k), after))
        after = move_row(plan[1 + k], merge(*near[k][:2], mine))
        moved.append(after)

    outgoing, kept = pack(plan, ids, norm_gain.reshape(1, features), moved[0], moved[1], experts * rows * CAP)
    arrived = lax.all_to_all(
        outgoing.reshape(experts, rows * CAP, features), "expert", split_axis=0, concat_axis=0, tiled=True
    )
    produced = ffn(
        arrived.reshape(-1, features),
        jnp.swapaxes(expert_gate, 1, 2)[0],
        jnp.swapaxes(expert_up, 1, 2)[0],
        expert_down[0],
    )
    returned = lax.all_to_all(
        produced.reshape(experts, rows * CAP, features), "expert", split_axis=0, concat_axis=0, tiled=True
    )
    return combine(plan, ids, kept, returned.reshape(-1, features), rows)


def solution(mesh):
    in_specs = (
        P("dp", "expert", None),
        P("dp", "expert", None),
        P("dp", "expert", None),
        P(),
        P(),
        P("dp", "expert", None),
        P(),
        P("expert", None, None),
        P("expert", None, None),
        P("expert", None, None),
    )
    return jax.shard_map(
        on_device,
        mesh=mesh,
        in_specs=in_specs,
        out_specs=P("dp", "expert", None),
        check_vma=False,
    )
```

```python
import functools
import itertools
import math

import jax
import jax.numpy as jnp
from jax import lax
from jax.experimental import pallas as pl
from jax.experimental.pallas import tpu as pltpu
from jax.sharding import PartitionSpec as P

HEADS = 16
HDIM = 128
CAP = 4
EXT = 128
SPLITS = ((16,), (16,))
NEG = -1e30
SCALE = math.log2(math.e) / math.sqrt(HDIM)
NT = (((1,), (1,)), ((), ()))
VMEM = pl.BlockSpec(memory_space=pltpu.VMEM)
SMEM = pl.BlockSpec(memory_space=pltpu.SMEM)
ANY = pl.BlockSpec(memory_space=pl.ANY)
MIB = 1 << 20
PERMS = 24
PLAN_MIB = 8
FFN_MIB = 20


def params(mib):
    return pltpu.CompilerParams(vmem_limit_bytes=mib * MIB)


def cost(flops, nbytes, exps=0):
    return pl.CostEstimate(flops=flops, bytes_accessed=nbytes, transcendentals=exps)


def parts_of(splits):
    for k, heads in enumerate(splits):
        first = 0
        for count in heads:
            yield k, slice(first * HDIM, (first + count) * HDIM)
            first += count


PARTS = tuple(parts_of(SPLITS))


def of_row(values, which):
    return [value for value, (k, _) in zip(values, PARTS) if k == which]


def plan_kernel(target_ref, q_ref, plan_ref, *refs):
    piece_refs, sems = refs[:-1], refs[-1]
    group = lax.axis_index("dp")
    to_group = [target_ref[r] // 2 for r in range(8)]
    weight = [jnp.left_shift(1, t) for t in to_group]
    picked = jnp.int32(-1)
    for choice in reversed(range(8)):
        bits = [0, choice & 1, (choice >> 1) & 1, (choice >> 2) & 1]
        total = sum(weight[2 * g + bits[g]] for g in range(4))
        picked = jnp.where(total == 15, choice, picked)
    picked = jnp.maximum(picked, 0)
    first = [jnp.int32(0), picked & 1, (picked >> 1) & 1, (picked >> 2) & 1]
    mine = jnp.int32(0)
    for g in range(4):
        mine = jnp.where(group == g, first[g], mine)
    copies = []
    for i, (k, cols) in enumerate(PARTS):
        row = mine if k == 0 else 1 - mine
        copies.append(pltpu.make_async_copy(q_ref.at[row, :, cols], piece_refs[i], sems.at[i]))
        copies[-1].start()
    given = [
        [jnp.where(first[g] == 0, to_group[2 * g], to_group[2 * g + 1]) for g in range(4)],
        [jnp.where(first[g] == 0, to_group[2 * g + 1], to_group[2 * g]) for g in range(4)],
    ]
    slot = jnp.int32(0)
    for g in range(4):
        row_slot = jnp.where(first[g] == 0, target_ref[2 * g], target_ref[2 * g + 1]) % 2
        slot = jnp.where(given[0][g] == group, row_slot, slot)
    plan_ref[0] = mine
    for k in range(2):
        p = given[k]
        second = p[1] - (p[1] > p[0]).astype(jnp.int32)
        plan_ref[1 + k] = 6 * p[0] + 2 * second + (p[2] > p[3]).astype(jnp.int32)
    plan_ref[3] = slot
    for i in range(4, 8):
        plan_ref[i] = 0
    for copy in copies:
        copy.wait()


def make_plan(row_target, queries):
    _, width, _ = queries.shape
    pieces = [jax.ShapeDtypeStruct((width, c.stop - c.start), queries.dtype) for _, c in PARTS]
    return pl.pallas_call(
        plan_kernel,
        out_shape=[jax.ShapeDtypeStruct((8,), jnp.int32)] + pieces,
        in_specs=[SMEM, ANY],
        out_specs=[SMEM] + [VMEM] * len(pieces),
        scratch_shapes=[pltpu.SemaphoreType.DMA((len(pieces),))],
        compiler_params=params(PLAN_MIB),
        cost_estimate=cost(0, 4 * MIB),
    )(row_target, queries)


def contig_start_of(lengths, query_pos):
    n = lengths.shape[1]
    above = lax.broadcasted_iota(jnp.int32, (n, n), 0)
    along = lax.broadcasted_iota(jnp.int32, (n, n), 1)
    spread = jnp.broadcast_to(lengths, (n, n))
    column = jnp.sum(jnp.where(above == along, spread, 0), axis=1, keepdims=True)
    ends = jnp.sum(jnp.where(above <= along, jnp.broadcast_to(column, (n, n)), 0), axis=0, keepdims=True)
    return jnp.sum(jnp.where(ends <= query_pos, lengths, 0), axis=1, keepdims=True)


def attend(lengths, q_ref, k_ref, v_ref, ahead, rounded_peak, write):
    width = q_ref.shape[0]
    shard = lax.axis_index("expert")
    first = (shard + ahead) * width
    start = contig_start_of(lengths, first + lax.broadcasted_iota(jnp.int32, (width, 1), 0))
    query_pos = first + lax.broadcasted_iota(jnp.int32, (width, 2 * width), 0)
    lane = lax.broadcasted_iota(jnp.int32, (width, 2 * width), 1)
    pair = shard + 1 - 2 * (shard % 2)
    key_pos = jnp.where(lane < width, shard * width + lane, (pair - 1) * width + lane)
    bias = jnp.where((key_pos >= start) & (key_pos <= query_pos), 0.0, NEG)
    peaks, totals = [], []
    for h in range(q_ref.shape[1] // HDIM):
        cols = slice(h * HDIM, (h + 1) * HDIM)
        scores = lax.dot_general(q_ref[:, cols], k_ref[:, cols], NT, preferred_element_type=jnp.float32)
        scores = scores * SCALE + bias
        peak = jnp.maximum(jnp.max(scores, axis=1, keepdims=True), NEG * 0.1)
        if rounded_peak:
            peak = peak.astype(jnp.bfloat16).astype(jnp.float32)
        probs = jnp.exp2(scores - peak)
        totals.append(jnp.sum(probs, axis=1, keepdims=True))
        peaks.append(peak)
        write(h, jnp.dot(probs.astype(jnp.bfloat16), v_ref[:, cols], preferred_element_type=jnp.float32))
    return peaks, totals


def spread_columns(columns_at, shape):
    lane = lax.broadcasted_iota(jnp.int32, shape, 1)
    out = jnp.zeros(shape, jnp.float32)
    for at, column in columns_at:
        out = jnp.where(lane == at, column, out)
    return out


def own_row(len_ref, row):
    return len_ref[pl.ds(lax.axis_index("dp") * 2 + row, 1), :]


def near_kernel(
    which, plan_ref, len_ref, ko_ref, kp_ref, vo_ref, vp_ref, *refs
):
    q_refs, (sums_ref, stats_ref, k_ref, v_ref) = refs[:-4], refs[-4:]
    row = plan_ref[0] if which == 0 else 1 - plan_ref[0]
    width = q_refs[0].shape[0]
    for both, own, pair in ((k_ref, ko_ref, kp_ref), (v_ref, vo_ref, vp_ref)):
        both[:width, :] = own[row]
        both[width:, :] = pair[row]
    columns = []
    for q_ref, cols in zip(q_refs, [c for k, c in PARTS if k == which]):

        def write(h, sums):
            sums_ref[:, cols.start + h * HDIM:cols.start + (h + 1) * HDIM] = sums

        peaks, totals = attend(
            own_row(len_ref, row), q_ref, k_ref.at[:, cols], v_ref.at[:, cols], 0, False, write
        )
        for h, (peak, total) in enumerate(zip(peaks, totals)):
            at = cols.start // HDIM + h
            columns += [(at, peak), (HEADS + at, total)]
    stats_ref[...] = spread_columns(columns, stats_ref.shape)


def near_attention(which, plan, lengths, pieces, k_own, k_pair, v_own, v_pair):
    _, width, features = k_own.shape
    both = jax.ShapeDtypeStruct((2 * width, features), k_own.dtype)
    return pl.pallas_call(
        functools.partial(near_kernel, which),
        out_shape=[
            jax.ShapeDtypeStruct((width, features), jnp.float32),
            jax.ShapeDtypeStruct((width, EXT), jnp.float32),
            both,
            both,
        ],
        in_specs=[SMEM] + [VMEM] * (4 + 1 + len(pieces)),
        out_specs=[VMEM] * 4,
        compiler_params=params(20),
        cost_estimate=cost(4 * width * 2 * width * features, 6 * MIB, HEADS * 2 * width * width),
    )(plan, lengths, k_own, k_pair, v_own, v_pair, *pieces)


def far_kernel(index, plan_ref, len_ref, q_ref, k_ref, v_ref, out_ref):
    row = plan_ref[0] if PARTS[index][0] == 0 else 1 - plan_ref[0]
    width, step = q_ref.shape
    cols = PARTS[index][1]

    def write(h, sums):
        out_ref[:, h * HDIM:(h + 1) * HDIM] = sums.astype(jnp.bfloat16)

    peaks, totals = attend(
        own_row(len_ref, row), q_ref, k_ref.at[:, cols], v_ref.at[:, cols], 2, True, write
    )
    columns = []
    for h, (peak, total) in enumerate(zip(peaks, totals)):
        high = total.astype(jnp.bfloat16).astype(jnp.float32)
        columns += [(h, peak), (HEADS + h, high), (2 * HEADS + h, total - high)]
    out_ref[:, step:] = spread_columns(columns, (width, EXT)).astype(jnp.bfloat16)


def far_attention(index, plan, lengths, q, k, v):
    width, step = q.shape
    return pl.pallas_call(
        functools.partial(far_kernel, index),
        out_shape=jax.ShapeDtypeStruct((width, step + EXT), jnp.bfloat16),
        in_specs=[SMEM, VMEM, VMEM, VMEM, VMEM],
        out_specs=VMEM,
        compiler_params=params(12),
        cost_estimate=cost(4 * width * 2 * width * step, 3 * MIB, step // HDIM * 2 * width * width),
    )(plan, lengths, q, k, v)


def merge_kernel(sums_ref, stats_ref, *refs):
    far_refs, out_ref = refs[:-1], refs[-1]
    first = 0
    for far_ref in far_refs:
        step = far_ref.shape[1] - EXT
        count = step // HDIM
        peak = stats_ref[:, first:first + count]
        total = stats_ref[:, HEADS + first:HEADS + first + count]
        far_stats = far_ref[:, step:].astype(jnp.float32)
        far_peak = far_stats[:, :count]
        far_total = far_stats[:, HEADS:HEADS + count] + far_stats[:, 2 * HEADS:2 * HEADS + count]
        some = far_total > 0
        top = jnp.maximum(peak, jnp.where(some, far_peak, NEG))
        share = jnp.exp2(peak - top)
        far_share = jnp.where(some, jnp.exp2(far_peak - top), 0.0)
        whole = total * share + far_total * far_share
        share, far_share = share / whole, far_share / whole
        for h in range(count):
            cols = slice((first + h) * HDIM, (first + h + 1) * HDIM)
            mixed = sums_ref[:, cols] * share[:, h:h + 1]
            mixed += far_ref[:, h * HDIM:(h + 1) * HDIM].astype(jnp.float32) * far_share[:, h:h + 1]
            out_ref[:, cols] = mixed.astype(jnp.bfloat16)
        first += count


def merge(sums, stats, far):
    width, features = sums.shape
    return pl.pallas_call(
        merge_kernel,
        out_shape=jax.ShapeDtypeStruct((width, features), jnp.bfloat16),
        in_specs=[VMEM] * (2 + len(far)),
        out_specs=VMEM,
        compiler_params=params(8),
        cost_estimate=cost(4 * width * features, 2 * MIB),
    )(sums, stats, *far)


def move_row(index, value):
    count = lax.axis_size("dp")
    branches = [
        functools.partial(lax.ppermute, axis_name="dp", perm=list(enumerate(perm)))
        for perm in itertools.permutations(range(count))
    ]
    return lax.switch(index, branches, value)


def around(value, steps):
    count = lax.axis_size("expert")
    return lax.ppermute(value, "expert", [(i, (i + steps) % count) for i in range(count)])


def other_core(value):
    count = lax.axis_size("expert")
    return lax.ppermute(value, "expert", [(i, i ^ 1) for i in range(count)])


def slots_of(ids, round_index):
    w = ids.shape[1]
    above = lax.broadcasted_iota(jnp.int32, (w, w), 0)
    along = lax.broadcasted_iota(jnp.int32, (w, w), 1)
    spread = jnp.broadcast_to(ids, (w, w))
    column = jnp.sum(jnp.where(above == along, spread, 0), axis=1, keepdims=True)
    rank = jnp.sum(jnp.where((column == spread) & (above < along), 1, 0), axis=0, keepdims=True)
    return ids * (2 * CAP) + round_index * CAP + rank


def all_slots(plan_ref, ids_ref):
    slot = plan_ref[3]
    return [slots_of(ids_ref[pl.ds(row, 1), :], k) for k, row in enumerate((slot, 1 - slot))]


def pack_kernel(plan_ref, ids_ref, gain_ref, a_hbm, b_hbm, out_ref, kept_ref, normed_ref, sems):
    width, features = a_hbm.shape
    copies = [
        pltpu.make_async_copy(hbm, kept_ref.at[k * width:(k + 1) * width], sems.at[k])
        for k, hbm in enumerate((a_hbm, b_hbm))
    ]
    for copy in copies:
        copy.start()
    slots = jnp.concatenate(all_slots(plan_ref, ids_ref), axis=1)
    count = out_ref.shape[0]
    table = (lax.broadcasted_iota(jnp.int32, (count, 2 * width), 0) == slots).astype(jnp.float32)
    table = table.astype(jnp.bfloat16)
    gain = gain_ref[...]
    for k, copy in enumerate(copies):
        copy.wait()
        rows = slice(k * width, (k + 1) * width)
        hidden = kept_ref[rows, :].astype(jnp.float32)
        mean_square = jnp.sum(hidden * hidden, axis=1, keepdims=True) * (1.0 / features)
        normed = hidden * lax.rsqrt(mean_square + 1e-05) * gain
        normed_ref[rows, :] = normed.astype(jnp.bfloat16)
    for c in range(0, features, 512):
        out_ref[:, c:c + 512] = jnp.dot(
            table, normed_ref[:, c:c + 512], preferred_element_type=jnp.float32
        ).astype(jnp.bfloat16)


def pack(plan, ids, gain, a, b, count):
    width, features = a.shape
    return pl.pallas_call(
        pack_kernel,
        out_shape=[
            jax.ShapeDtypeStruct((count, features), jnp.bfloat16),
            jax.ShapeDtypeStruct((2 * width, features), jnp.bfloat16),
        ],
        in_specs=[SMEM, VMEM, VMEM, ANY, ANY],
        out_specs=[VMEM, VMEM],
        scratch_shapes=[
            pltpu.VMEM((2 * width, features), jnp.bfloat16),
            pltpu.SemaphoreType.DMA((2,)),
        ],
        compiler_params=params(16),
        cost_estimate=cost(4 * count * width * features, 3 * MIB),
    )(plan, ids, gain, a, b)


def up_kernel(x_ref, gate_ref, up_ref, act_ref):
    hidden = gate_ref.shape[0]
    x = x_ref[...]
    for c in range(0, hidden, 256):
        rows = slice(c, min(c + 256, hidden))
        gate = lax.dot_general(x, gate_ref[rows, :], NT, preferred_element_type=jnp.float32)
        up = lax.dot_general(x, up_ref[rows, :], NT, preferred_element_type=jnp.float32)
        act_ref[:, rows] = (gate / (1.0 + jnp.exp(-gate)) * up).astype(jnp.bfloat16)


def down_kernel(act_ref, down_ref, out_ref):
    act = act_ref[...]
    for c in range(0, down_ref.shape[1], 512):
        out_ref[:, c:c + 512] = jnp.dot(
            act, down_ref[:, c:c + 512], preferred_element_type=jnp.float32
        ).astype(jnp.bfloat16)


def ffn(x, gate, up, down):
    count, features = x.shape
    hidden = down.shape[0]
    act = pl.pallas_call(
        up_kernel,
        out_shape=jax.ShapeDtypeStruct((count, hidden), jnp.bfloat16),
        in_specs=[VMEM] * 3,
        out_specs=VMEM,
        compiler_params=params(FFN_MIB),
        cost_estimate=cost(4 * count * hidden * features, 12 * MIB, count * hidden),
    )(x, gate, up)
    return pl.pallas_call(
        down_kernel,
        out_shape=jax.ShapeDtypeStruct((count, features), jnp.bfloat16),
        in_specs=[VMEM] * 2,
        out_specs=VMEM,
        compiler_params=params(FFN_MIB),
        cost_estimate=cost(2 * count * hidden * features, 6 * MIB),
    )(act, down)


def combine_kernel(plan_ref, ids_ref, kept_ref, got_ref, out_hbm, out_ref, sems):
    rows, width, features = out_hbm.shape
    slot = plan_ref[3]
    above = lax.broadcasted_iota(jnp.int32, (width, width), 0)
    along = lax.broadcasted_iota(jnp.int32, (width, width), 1)
    place = lax.broadcasted_iota(jnp.int32, (width, got_ref.shape[0]), 1)
    tables = []
    for slots in all_slots(plan_ref, ids_ref):
        column = jnp.sum(jnp.where(above == along, slots, 0), axis=1, keepdims=True)
        tables.append((place == column).astype(jnp.float32).astype(jnp.bfloat16))
    table = jnp.concatenate(tables, axis=0)
    copies = []
    for i, c in enumerate(range(0, features, 512)):
        cols = slice(c, c + 512)
        chosen = jnp.dot(table, got_ref[:, cols], preferred_element_type=jnp.float32)
        total = (kept_ref[:, cols].astype(jnp.float32) + chosen).astype(jnp.bfloat16)
        out_ref[slot, :, cols] = total[:width]
        out_ref[1 - slot, :, cols] = total[width:]
        copies.append(pltpu.make_async_copy(out_ref.at[:, :, cols], out_hbm.at[:, :, cols], sems.at[i]))
        copies[-1].start()
    for copy in copies:
        copy.wait()


def combine(plan, ids, kept, got, rows):
    count, features = got.shape
    width = kept.shape[0] // rows
    return pl.pallas_call(
        combine_kernel,
        out_shape=jax.ShapeDtypeStruct((rows, width, features), jnp.bfloat16),
        in_specs=[SMEM, VMEM, VMEM, VMEM],
        out_specs=ANY,
        scratch_shapes=[
            pltpu.VMEM((rows, width, features), jnp.bfloat16),
            pltpu.SemaphoreType.DMA((features // 512,)),
        ],
        compiler_params=params(16),
        cost_estimate=cost(4 * count * width * features, 4 * MIB),
    )(plan, ids, kept, got)


def on_device(
    queries,
    key_rows,
    value_rows,
    contig_lengths,
    row_target,
    species_expert,
    norm_gain,
    expert_gate,
    expert_up,
    expert_down,
):
    rows, width, features = queries.shape
    experts = expert_gate.shape[0] * lax.axis_size("expert")
    ids = species_expert.reshape(rows, width)

    plan, *pieces = make_plan(row_target, queries)
    far_q = [around(piece, -2) for piece in pieces]
    k_pair, v_pair = other_core(key_rows), other_core(value_rows)
    near = [
        near_attention(
            k, plan, contig_lengths, of_row(pieces, k), key_rows, k_pair, value_rows, v_pair
        )
        for k in range(2)
    ]
    perms = [lax.clamp(0, plan[1 + k], PERMS - 1) for k in range(2)]
    far_q[0], near = lax.optimization_barrier((far_q[0], near))
    far_q[0], _ = lax.optimization_barrier((far_q[0], perms))
    far, back = [], []
    for i, q in enumerate(far_q):
        k = PARTS[i][0]
        if i:
            q, _ = lax.optimization_barrier((q, far[-1]))
        far.append(far_attention(i, plan, contig_lengths, q, *near[k][2:]))
        back.append(around(far[-1], 2))
    moved = []
    after = far[-1]
    for k in range(2):
        mine, _ = lax.optimization_barrier((of_row(back, k), after))
        after = move_row(plan[1 + k], merge(*near[k][:2], mine))
        moved.append(after)

    outgoing, kept = pack(plan, ids, norm_gain.reshape(1, features), moved[0], moved[1], experts * rows * CAP)
    arrived = lax.all_to_all(
        outgoing.reshape(experts, rows * CAP, features), "expert", split_axis=0, concat_axis=0, tiled=True
    )
    produced = ffn(
        arrived.reshape(-1, features),
        jnp.swapaxes(expert_gate, 1, 2)[0],
        jnp.swapaxes(expert_up, 1, 2)[0],
        expert_down[0],
    )
    returned = lax.all_to_all(
        produced.reshape(experts, rows * CAP, features), "expert", split_axis=0, concat_axis=0, tiled=True
    )
    return combine(plan, ids, kept, returned.reshape(-1, features), rows)


def solution(mesh):
    in_specs = (
        P("dp", "expert", None),
        P("dp", "expert", None),
        P("dp", "expert", None),
        P(),
        P(),
        P("dp", "expert", None),
        P(),
        P("expert", None, None),
        P("expert", None, None),
        P("expert", None, None),
    )
    return jax.shard_map(
        on_device,
        mesh=mesh,
        in_specs=in_specs,
        out_specs=P("dp", "expert", None),
        check_vma=False,
    )
```

```python
import functools
import itertools
import math

import jax
import jax.numpy as jnp
from jax import lax
from jax.experimental import pallas as pl
from jax.experimental.pallas import tpu as pltpu
from jax.sharding import PartitionSpec as P

HEADS = 16
HDIM = 128
CAP = 4
EXT = 128
SPLITS = ((16,), (16,))
NEG = -1e30
SCALE = math.log2(math.e) / math.sqrt(HDIM)
NT = (((1,), (1,)), ((), ()))
VMEM = pl.BlockSpec(memory_space=pltpu.VMEM)
SMEM = pl.BlockSpec(memory_space=pltpu.SMEM)
ANY = pl.BlockSpec(memory_space=pl.ANY)
MIB = 1 << 20
PERMS = 24
PLAN_MIB = 8
FFN_MIB = 20


def params(mib):
    return pltpu.CompilerParams(vmem_limit_bytes=mib * MIB)


def cost(flops, nbytes, exps=0):
    return pl.CostEstimate(flops=flops, bytes_accessed=nbytes, transcendentals=exps)


def parts_of(splits):
    for k, heads in enumerate(splits):
        first = 0
        for count in heads:
            yield k, slice(first * HDIM, (first + count) * HDIM)
            first += count


PARTS = tuple(parts_of(SPLITS))


def of_row(values, which):
    return [value for value, (k, _) in zip(values, PARTS) if k == which]


def plan_kernel(target_ref, q_ref, k_ref, v_ref, plan_ref, *refs):
    piece_refs, sems = refs[:-1], refs[-1]
    group = lax.axis_index("dp")
    to_group = [target_ref[r] // 2 for r in range(8)]
    weight = [jnp.left_shift(1, t) for t in to_group]
    picked = jnp.int32(-1)
    for choice in reversed(range(8)):
        bits = [0, choice & 1, (choice >> 1) & 1, (choice >> 2) & 1]
        total = sum(weight[2 * g + bits[g]] for g in range(4))
        picked = jnp.where(total == 15, choice, picked)
    picked = jnp.maximum(picked, 0)
    first = [jnp.int32(0), picked & 1, (picked >> 1) & 1, (picked >> 2) & 1]
    mine = jnp.int32(0)
    for g in range(4):
        mine = jnp.where(group == g, first[g], mine)
    copies = []
    for i, (k, cols) in enumerate(PARTS):
        row = mine if k == 0 else 1 - mine
        copies.append(pltpu.make_async_copy(q_ref.at[row, :, cols], piece_refs[i], sems.at[i]))
        width = q_ref.shape[1]
        for j, ref in enumerate((k_ref, v_ref)):
            to = piece_refs[2 + i].at[j * width:(j + 1) * width]
            copies.append(pltpu.make_async_copy(ref.at[row], to, sems.at[2 + 2 * i + j]))
    for copy in copies:
        copy.start()
    given = [
        [jnp.where(first[g] == 0, to_group[2 * g], to_group[2 * g + 1]) for g in range(4)],
        [jnp.where(first[g] == 0, to_group[2 * g + 1], to_group[2 * g]) for g in range(4)],
    ]
    slot = jnp.int32(0)
    for g in range(4):
        row_slot = jnp.where(first[g] == 0, target_ref[2 * g], target_ref[2 * g + 1]) % 2
        slot = jnp.where(given[0][g] == group, row_slot, slot)
    plan_ref[0] = mine
    for k in range(2):
        p = given[k]
        second = p[1] - (p[1] > p[0]).astype(jnp.int32)
        plan_ref[1 + k] = 6 * p[0] + 2 * second + (p[2] > p[3]).astype(jnp.int32)
    plan_ref[3] = slot
    for i in range(4, 8):
        plan_ref[i] = 0
    for copy in copies:
        copy.wait()


def make_plan(row_target, queries, keys, values):
    _, width, _ = queries.shape
    pieces = [jax.ShapeDtypeStruct((width, c.stop - c.start), queries.dtype) for _, c in PARTS]
    pieces += [jax.ShapeDtypeStruct((2 * width, c.stop - c.start), queries.dtype) for _, c in PARTS]
    return pl.pallas_call(
        plan_kernel,
        out_shape=[jax.ShapeDtypeStruct((8,), jnp.int32)] + pieces,
        in_specs=[SMEM, ANY, ANY, ANY],
        out_specs=[SMEM] + [VMEM] * len(pieces),
        scratch_shapes=[pltpu.SemaphoreType.DMA((6,))],
        compiler_params=params(PLAN_MIB),
        cost_estimate=cost(0, 4 * MIB),
    )(row_target, queries, keys, values)


def contig_start_of(lengths, query_pos):
    n = lengths.shape[1]
    above = lax.broadcasted_iota(jnp.int32, (n, n), 0)
    along = lax.broadcasted_iota(jnp.int32, (n, n), 1)
    spread = jnp.broadcast_to(lengths, (n, n))
    column = jnp.sum(jnp.where(above == along, spread, 0), axis=1, keepdims=True)
    ends = jnp.sum(jnp.where(above <= along, jnp.broadcast_to(column, (n, n)), 0), axis=0, keepdims=True)
    return jnp.sum(jnp.where(ends <= query_pos, lengths, 0), axis=1, keepdims=True)


def attend(lengths, q_ref, k_ref, v_ref, ahead, rounded_peak, write, behind=0):
    width = q_ref.shape[0]
    shard = lax.axis_index("expert")
    first = (shard + ahead) * width
    start = contig_start_of(lengths, first + lax.broadcasted_iota(jnp.int32, (width, 1), 0))
    keys = k_ref.shape[0]
    query_pos = first + lax.broadcasted_iota(jnp.int32, (width, keys), 0)
    lane = lax.broadcasted_iota(jnp.int32, (width, keys), 1)
    pair = shard + 1 - 2 * (shard % 2)
    key_pos = jnp.where(lane < width, (shard - behind) * width + lane, (pair - 1) * width + lane)
    bias = jnp.where((key_pos >= start) & (key_pos <= query_pos), 0.0, NEG)
    peaks, totals = [], []
    for h in range(q_ref.shape[1] // HDIM):
        cols = slice(h * HDIM, (h + 1) * HDIM)
        scores = lax.dot_general(q_ref[:, cols], k_ref[:, cols], NT, preferred_element_type=jnp.float32)
        scores = scores * SCALE + bias
        peak = jnp.maximum(jnp.max(scores, axis=1, keepdims=True), NEG * 0.1)
        if rounded_peak:
            peak = peak.astype(jnp.bfloat16).astype(jnp.float32)
        probs = jnp.exp2(scores - peak)
        totals.append(jnp.sum(probs, axis=1, keepdims=True))
        peaks.append(peak)
        write(h, jnp.dot(probs.astype(jnp.bfloat16), v_ref[:, cols], preferred_element_type=jnp.float32))
    return peaks, totals


def spread_columns(columns_at, shape):
    lane = lax.broadcasted_iota(jnp.int32, shape, 1)
    out = jnp.zeros(shape, jnp.float32)
    for at, column in columns_at:
        out = jnp.where(lane == at, column, out)
    return out


def own_row(len_ref, row):
    return len_ref[pl.ds(lax.axis_index("dp") * 2 + row, 1), :]


def near_kernel(
    which, plan_ref, len_ref, ko_ref, kp_ref, vo_ref, vp_ref, *refs
):
    q_refs, (sums_ref, stats_ref, k_ref, v_ref) = refs[:-4], refs[-4:]
    row = plan_ref[0] if which == 0 else 1 - plan_ref[0]
    width = q_refs[0].shape[0]
    for both, own, pair in ((k_ref, ko_ref, kp_ref), (v_ref, vo_ref, vp_ref)):
        both[:width, :] = own[row]
        both[width:, :] = pair[row]
    columns = []
    for q_ref, cols in zip(q_refs, [c for k, c in PARTS if k == which]):

        def write(h, sums):
            sums_ref[:, cols.start + h * HDIM:cols.start + (h + 1) * HDIM] = sums

        peaks, totals = attend(
            own_row(len_ref, row), q_ref, k_ref.at[:, cols], v_ref.at[:, cols], 0, False, write
        )
        for h, (peak, total) in enumerate(zip(peaks, totals)):
            at = cols.start // HDIM + h
            columns += [(at, peak), (HEADS + at, total)]
    stats_ref[...] = spread_columns(columns, stats_ref.shape)


def near_attention(which, plan, lengths, pieces, k_own, k_pair, v_own, v_pair):
    _, width, features = k_own.shape
    both = jax.ShapeDtypeStruct((2 * width, features), k_own.dtype)
    return pl.pallas_call(
        functools.partial(near_kernel, which),
        out_shape=[
            jax.ShapeDtypeStruct((width, features), jnp.float32),
            jax.ShapeDtypeStruct((width, EXT), jnp.float32),
            both,
            both,
        ],
        in_specs=[SMEM] + [VMEM] * (4 + 1 + len(pieces)),
        out_specs=[VMEM] * 4,
        compiler_params=params(20),
        cost_estimate=cost(4 * width * 2 * width * features, 6 * MIB, HEADS * 2 * width * width),
    )(plan, lengths, k_own, k_pair, v_own, v_pair, *pieces)


def far_kernel(which, plan_ref, len_ref, q_ref, k_ref, v_ref, own_q_ref, came_ref, out_ref):
    row = plan_ref[0] if which == 0 else 1 - plan_ref[0]
    width, step = q_ref.shape
    lengths = own_row(len_ref, row)
    second_core = lax.axis_index("expert") % 2 == 1

    def write(h, sums):
        out_ref[:, h * HDIM:(h + 1) * HDIM] = sums.astype(jnp.bfloat16)

    def finish(peaks, totals):
        columns = []
        for h, (peak, total) in enumerate(zip(peaks, totals)):
            high = total.astype(jnp.bfloat16).astype(jnp.float32)
            columns += [(h, peak), (HEADS + h, high), (2 * HEADS + h, total - high)]
        out_ref[:, step:] = spread_columns(columns, (width, EXT)).astype(jnp.bfloat16)

    @pl.when(jnp.logical_not(second_core))
    def _():
        finish(*attend(lengths, q_ref, k_ref, v_ref, 2, True, write))

    @pl.when(second_core)
    def _():
        keys, values = came_ref.at[:width], came_ref.at[width:]
        finish(*attend(lengths, own_q_ref, keys, values, 0, True, write, behind=2))


def far_attention(which, plan, lengths, q, k, v, own_q, came):
    width, step = q.shape
    return pl.pallas_call(
        functools.partial(far_kernel, which),
        out_shape=jax.ShapeDtypeStruct((width, step + EXT), jnp.bfloat16),
        in_specs=[SMEM] + [VMEM] * 6,
        out_specs=VMEM,
        compiler_params=params(12),
        cost_estimate=cost(4 * width * 2 * width * step, 3 * MIB, step // HDIM * 2 * width * width),
    )(plan, lengths, q, k, v, own_q, came)


def merge_kernel(sums_ref, stats_ref, own_ref, came_ref, out_ref):
    second_core = lax.axis_index("expert") % 2 == 1
    first = 0
    for _ in range(1):
        step = own_ref.shape[1] - EXT
        far_ref = jnp.where(second_core, own_ref[...], came_ref[...])
        count = step // HDIM
        peak = stats_ref[:, first:first + count]
        total = stats_ref[:, HEADS + first:HEADS + first + count]
        far_stats = far_ref[:, step:].astype(jnp.float32)
        far_peak = far_stats[:, :count]
        far_total = far_stats[:, HEADS:HEADS + count] + far_stats[:, 2 * HEADS:2 * HEADS + count]
        some = far_total > 0
        top = jnp.maximum(peak, jnp.where(some, far_peak, NEG))
        share = jnp.exp2(peak - top)
        far_share = jnp.where(some, jnp.exp2(far_peak - top), 0.0)
        whole = total * share + far_total * far_share
        share, far_share = share / whole, far_share / whole
        for h in range(count):
            cols = slice((first + h) * HDIM, (first + h + 1) * HDIM)
            mixed = sums_ref[:, cols] * share[:, h:h + 1]
            mixed += far_ref[:, h * HDIM:(h + 1) * HDIM].astype(jnp.float32) * far_share[:, h:h + 1]
            out_ref[:, cols] = mixed.astype(jnp.bfloat16)
        first += count


def merge(sums, stats, far):
    width, features = sums.shape
    return pl.pallas_call(
        merge_kernel,
        out_shape=jax.ShapeDtypeStruct((width, features), jnp.bfloat16),
        in_specs=[VMEM] * 4,
        out_specs=VMEM,
        compiler_params=params(8),
        cost_estimate=cost(4 * width * features, 2 * MIB),
    )(sums, stats, *far)


def move_row(index, value):
    count = lax.axis_size("dp")
    branches = [
        functools.partial(lax.ppermute, axis_name="dp", perm=list(enumerate(perm)))
        for perm in itertools.permutations(range(count))
    ]
    return lax.switch(index, branches, value)


def around(value, steps, core):
    count = lax.axis_size("expert")
    pairs = [(i, (i + steps) % count) for i in range(core, count, 2)]
    return lax.ppermute(value, "expert", pairs)


def other_core(value):
    count = lax.axis_size("expert")
    return lax.ppermute(value, "expert", [(i, i ^ 1) for i in range(count)])


def slots_of(ids, round_index):
    w = ids.shape[1]
    above = lax.broadcasted_iota(jnp.int32, (w, w), 0)
    along = lax.broadcasted_iota(jnp.int32, (w, w), 1)
    spread = jnp.broadcast_to(ids, (w, w))
    column = jnp.sum(jnp.where(above == along, spread, 0), axis=1, keepdims=True)
    rank = jnp.sum(jnp.where((column == spread) & (above < along), 1, 0), axis=0, keepdims=True)
    return ids * (2 * CAP) + round_index * CAP + rank


def all_slots(plan_ref, ids_ref):
    slot = plan_ref[3]
    return [slots_of(ids_ref[pl.ds(row, 1), :], k) for k, row in enumerate((slot, 1 - slot))]


def pack_kernel(plan_ref, ids_ref, gain_ref, a_hbm, b_hbm, out_ref, kept_ref, normed_ref, sems):
    width, features = a_hbm.shape
    copies = [
        pltpu.make_async_copy(hbm, kept_ref.at[k * width:(k + 1) * width], sems.at[k])
        for k, hbm in enumerate((a_hbm, b_hbm))
    ]
    for copy in copies:
        copy.start()
    slots = jnp.concatenate(all_slots(plan_ref, ids_ref), axis=1)
    count = out_ref.shape[0]
    table = (lax.broadcasted_iota(jnp.int32, (count, 2 * width), 0) == slots).astype(jnp.float32)
    table = table.astype(jnp.bfloat16)
    gain = gain_ref[...]
    for k, copy in enumerate(copies):
        copy.wait()
        rows = slice(k * width, (k + 1) * width)
        hidden = kept_ref[rows, :].astype(jnp.float32)
        mean_square = jnp.sum(hidden * hidden, axis=1, keepdims=True) * (1.0 / features)
        normed = hidden * lax.rsqrt(mean_square + 1e-05) * gain
        normed_ref[rows, :] = normed.astype(jnp.bfloat16)
    for c in range(0, features, 512):
        out_ref[:, c:c + 512] = jnp.dot(
            table, normed_ref[:, c:c + 512], preferred_element_type=jnp.float32
        ).astype(jnp.bfloat16)


def pack(plan, ids, gain, a, b, count):
    width, features = a.shape
    return pl.pallas_call(
        pack_kernel,
        out_shape=[
            jax.ShapeDtypeStruct((count, features), jnp.bfloat16),
            jax.ShapeDtypeStruct((2 * width, features), jnp.bfloat16),
        ],
        in_specs=[SMEM, VMEM, VMEM, ANY, ANY],
        out_specs=[VMEM, VMEM],
        scratch_shapes=[
            pltpu.VMEM((2 * width, features), jnp.bfloat16),
            pltpu.SemaphoreType.DMA((2,)),
        ],
        compiler_params=params(16),
        cost_estimate=cost(4 * count * width * features, 3 * MIB),
    )(plan, ids, gain, a, b)


def up_kernel(x_ref, gate_ref, up_ref, act_ref):
    hidden = gate_ref.shape[0]
    x = x_ref[...]
    for c in range(0, hidden, 256):
        rows = slice(c, min(c + 256, hidden))
        gate = lax.dot_general(x, gate_ref[rows, :], NT, preferred_element_type=jnp.float32)
        up = lax.dot_general(x, up_ref[rows, :], NT, preferred_element_type=jnp.float32)
        act_ref[:, rows] = (gate / (1.0 + jnp.exp(-gate)) * up).astype(jnp.bfloat16)


def down_kernel(act_ref, down_ref, out_ref):
    act = act_ref[...]
    for c in range(0, down_ref.shape[1], 512):
        out_ref[:, c:c + 512] = jnp.dot(
            act, down_ref[:, c:c + 512], preferred_element_type=jnp.float32
        ).astype(jnp.bfloat16)


def ffn(x, gate, up, down):
    count, features = x.shape
    hidden = down.shape[0]
    act = pl.pallas_call(
        up_kernel,
        out_shape=jax.ShapeDtypeStruct((count, hidden), jnp.bfloat16),
        in_specs=[VMEM] * 3,
        out_specs=VMEM,
        compiler_params=params(FFN_MIB),
        cost_estimate=cost(4 * count * hidden * features, 12 * MIB, count * hidden),
    )(x, gate, up)
    return pl.pallas_call(
        down_kernel,
        out_shape=jax.ShapeDtypeStruct((count, features), jnp.bfloat16),
        in_specs=[VMEM] * 2,
        out_specs=VMEM,
        compiler_params=params(FFN_MIB),
        cost_estimate=cost(2 * count * hidden * features, 6 * MIB),
    )(act, down)


def combine_kernel(plan_ref, ids_ref, kept_ref, got_ref, out_hbm, out_ref, sems):
    rows, width, features = out_hbm.shape
    slot = plan_ref[3]
    above = lax.broadcasted_iota(jnp.int32, (width, width), 0)
    along = lax.broadcasted_iota(jnp.int32, (width, width), 1)
    place = lax.broadcasted_iota(jnp.int32, (width, got_ref.shape[0]), 1)
    tables = []
    for slots in all_slots(plan_ref, ids_ref):
        column = jnp.sum(jnp.where(above == along, slots, 0), axis=1, keepdims=True)
        tables.append((place == column).astype(jnp.float32).astype(jnp.bfloat16))
    table = jnp.concatenate(tables, axis=0)
    copies = []
    for i, c in enumerate(range(0, features, 512)):
        cols = slice(c, c + 512)
        chosen = jnp.dot(table, got_ref[:, cols], preferred_element_type=jnp.float32)
        total = (kept_ref[:, cols].astype(jnp.float32) + chosen).astype(jnp.bfloat16)
        out_ref[slot, :, cols] = total[:width]
        out_ref[1 - slot, :, cols] = total[width:]
        copies.append(pltpu.make_async_copy(out_ref.at[:, :, cols], out_hbm.at[:, :, cols], sems.at[i]))
        copies[-1].start()
    for copy in copies:
        copy.wait()


def combine(plan, ids, kept, got, rows):
    count, features = got.shape
    width = kept.shape[0] // rows
    return pl.pallas_call(
        combine_kernel,
        out_shape=jax.ShapeDtypeStruct((rows, width, features), jnp.bfloat16),
        in_specs=[SMEM, VMEM, VMEM, VMEM],
        out_specs=ANY,
        scratch_shapes=[
            pltpu.VMEM((rows, width, features), jnp.bfloat16),
            pltpu.SemaphoreType.DMA((features // 512,)),
        ],
        compiler_params=params(16),
        cost_estimate=cost(4 * count * width * features, 4 * MIB),
    )(plan, ids, kept, got)


def on_device(
    queries,
    key_rows,
    value_rows,
    contig_lengths,
    row_target,
    species_expert,
    norm_gain,
    expert_gate,
    expert_up,
    expert_down,
):
    rows, width, features = queries.shape
    experts = expert_gate.shape[0] * lax.axis_size("expert")
    ids = species_expert.reshape(rows, width)

    plan, *pieces = make_plan(row_target, queries, key_rows, value_rows)
    pieces, both = pieces[:2], pieces[2:]
    far_q = [around(piece, -2, 0) for piece in pieces]
    came = [around(piece, 2, 1) for piece in both]
    k_pair, v_pair = other_core(key_rows), other_core(value_rows)
    near = [
        near_attention(
            k, plan, contig_lengths, of_row(pieces, k), key_rows, k_pair, value_rows, v_pair
        )
        for k in range(2)
    ]
    perms = [lax.clamp(0, plan[1 + k], PERMS - 1) for k in range(2)]
    far_q[0], near = lax.optimization_barrier((far_q[0], near))
    far_q[0], _ = lax.optimization_barrier((far_q[0], perms))
    far, back = [], []
    for i, q in enumerate(far_q):
        k = PARTS[i][0]
        if i:
            q, _ = lax.optimization_barrier((q, far[-1]))
        far.append(far_attention(i, plan, contig_lengths, q, *near[k][2:], pieces[i], came[i]))
        back.append(around(far[-1], 2, 0))
    moved = []
    after = far[-1]
    for k in range(2):
        mine, _ = lax.optimization_barrier((of_row(back, k), after))
        after = move_row(plan[1 + k], merge(*near[k][:2], [far[k]] + mine))
        moved.append(after)

    outgoing, kept = pack(plan, ids, norm_gain.reshape(1, features), moved[0], moved[1], experts * rows * CAP)
    arrived = lax.all_to_all(
        outgoing.reshape(experts, rows * CAP, features), "expert", split_axis=0, concat_axis=0, tiled=True
    )
    produced = ffn(
        arrived.reshape(-1, features),
        jnp.swapaxes(expert_gate, 1, 2)[0],
        jnp.swapaxes(expert_up, 1, 2)[0],
        expert_down[0],
    )
    returned = lax.all_to_all(
        produced.reshape(experts, rows * CAP, features), "expert", split_axis=0, concat_axis=0, tiled=True
    )
    return combine(plan, ids, kept, returned.reshape(-1, features), rows)


def solution(mesh):
    in_specs = (
        P("dp", "expert", None),
        P("dp", "expert", None),
        P("dp", "expert", None),
        P(),
        P(),
        P("dp", "expert", None),
        P(),
        P("expert", None, None),
        P("expert", None, None),
        P("expert", None, None),
    )
    return jax.shard_map(
        on_device,
        mesh=mesh,
        in_specs=in_specs,
        out_specs=P("dp", "expert", None),
        check_vma=False,
    )
```
